256 devices in a mesh: batch: 16 (over y, x), tensor: 16 (over z, core).
Axes of the slice: x: 4, y: 4, z: 8, core: 2. Of those that a mesh axis runs over, the one named last changes fastest.
Arguments:
- queries: bfloat16 [4, 256, 8192], P(None, 'batch', 'tensor'), may hold values from -130 to 130
- cache_keys: bfloat16 [256, 256, 16, 128], P('batch', None, 'tensor'), may hold values from -5 to 5, as said below
- cache_values: bfloat16 [256, 256, 16, 128], P('batch', None, 'tensor'), may hold values from -5 to 5, as said below
- new_keys: bfloat16 [4, 256, 16, 128], P(None, 'batch', 'tensor'), may hold values from -5 to 5, as said below
- new_values: bfloat16 [4, 256, 16, 128], P(None, 'batch', 'tensor'), may hold values from -5 to 5, as said below
- lengths: int32 [256], P('batch'), may hold values from 64 to 256, as said below
- admitted: int32 [4, 256], P(None, 'batch'), may hold values 0 or 1
- request_tenant: int32 [256], P('batch'), may hold values from 0 to 511, as said below
- tenant_adapter: int32 [512], replicated, may hold values from 0 to 127, as said below
- adapter_slot: int32 [128], replicated, may hold values from 0 to 127, as said below
- tenant_tokens: int32 [512], replicated, may hold values from 0 to 1023
- out_weight: bfloat16 [8192, 8192], P('tensor'), may hold values from -0.0625 to 0.0625
- adapter_down_factor: bfloat16 [128, 64, 8192], P('batch', None, 'tensor'), may hold values from -0.0625 to 0.0625
- adapter_up_factor: bfloat16 [128, 64, 8192], P('batch', None, 'tensor'), may hold values from -0.75 to 0.75
Outputs:
- outputs: bfloat16 [4, 256, 8192], P(None, 'batch', 'tensor')
The draws below stay inside these ranges and needn't reach their ends.
Inputs may be any that keep to these rules, and one draw needn't show every extreme that they name: `cache_keys`: every slot c holds an equal copy of key and value head c * 8 // 16. `cache_values`: every slot c holds an equal copy of key and value head c * 8 // 16. `new_keys`: every slot c holds an equal copy of key and value head c * 8 // 16. `new_values`: every slot c holds an equal copy of key and value head c * 8 // 16. `lengths`: some request has length 256. `tenant_adapter`: each tenant's adapter is named by exactly 4 tenants. A permutation: adapter a lies at row adapter_slot[a], stored with batch index adapter_slot[a] // 8. `request_tenant`: among the requests of one batch index, at most 2 have adapters stored with any one batch index; in every draw one batch index stores the adapters of exactly 2 requests of every batch index.
All inputs are finite; a program needn't handle non-finite values. No bound on the sum of `admitted` on one device may be relied on, other than what follows from the above.
Results may differ from the reference program's by a relative error of at most 0.0063.
Values may be sent and summed in bfloat16 or wider, within the bound.
No kernel may reach another device: no remote copies, remote signals or barrier semaphores. Data moves between devices by JAX's collectives and lax.ppermute only.
A program may use at most 64 MiB of HBM per device.

```python
import jax
import jax.numpy as jnp
from jax import lax

D = 8192
HQ = 64
KVH = 8
HD = 128
RANK = 64
REQ_DEV = 16
CTX = 256
STEPS = 4
REQUESTS = 256
CAP = 2
ADP_DEV = 8
ADAPTERS = 128
TENANTS = 512
KV_SLOTS = 16
HEADS_DEV = 4
LIMIT = 768
N_BATCH = 16


def widen(base_array):
    return jnp.repeat(base_array, KV_SLOTS // KVH, axis=2)


def cache_base(key):
    inner = jax.random.fold_in(key, 101)
    return jnp.clip(jax.random.normal(inner, (REQUESTS, CTX, KVH, HD), jnp.float32), -5.0, 5.0)


def fresh_base(key):
    inner = jax.random.fold_in(key, 102)
    return jnp.clip(jax.random.normal(inner, (STEPS, REQUESTS, KVH, HD), jnp.float32), -5.0, 5.0)


def routing(key):
    inner = jax.random.fold_in(key, 201)
    keys_list = jax.random.split(inner, 7)
    adapter_slot = jax.random.permutation(keys_list[0], ADAPTERS).astype(jnp.int32)
    tenant_perm = jax.random.permutation(keys_list[1], TENANTS).astype(jnp.int32)
    tenant_adapter = (tenant_perm % ADAPTERS).astype(jnp.int32)
    pool_size = N_BATCH * CAP
    pool = jnp.arange(pool_size, dtype=jnp.int32) // CAP
    favoured = jax.random.randint(keys_list[2], (1, 1), 0, N_BATCH)
    spread = jnp.arange(pool_size, dtype=jnp.int32)[None, :]
    random_rank = jax.random.randint(keys_list[3], (N_BATCH, pool_size), 0, 1 << 16)
    ranking = jnp.where(pool[None, :] == favoured, spread, pool_size + random_rank * pool_size + spread)
    picked = jnp.argsort(ranking, axis=1)[:, :REQ_DEV]
    holders = jnp.take(pool, picked)
    shuffle_rank = jax.random.randint(keys_list[4], (N_BATCH, REQ_DEV), 0, 1 << 16) * REQ_DEV + jnp.arange(REQ_DEV, dtype=jnp.int32)[None, :]
    holders = jnp.take_along_axis(holders, jnp.argsort(shuffle_rank, axis=1), axis=1).reshape(REQUESTS)
    within = jax.random.randint(keys_list[5], (REQUESTS,), 0, ADP_DEV)
    slot_needed = holders * ADP_DEV + within
    adapter_needed = jnp.take(jnp.argsort(adapter_slot), slot_needed)
    variant = jax.random.randint(keys_list[6], (REQUESTS,), 0, 2)
    request_tenant = jnp.take(jnp.argsort(tenant_perm), adapter_needed + ADAPTERS * variant).astype(jnp.int32)
    return (request_tenant, tenant_adapter, adapter_slot)


def draw_request_tenant(key, part):
    return routing(key)[0]


def draw_tenant_adapter(key, part):
    return routing(key)[1]


def draw_adapter_slot(key, part):
    return routing(key)[2]


def draw_lengths(key, part):
    key = jax.random.fold_in(key, 5)
    drawn = jax.random.randint(key, (REQUESTS,), CTX // 4, CTX + 1)
    return drawn.at[0].set(CTX).astype(jnp.int32)


def draw_cache_keys(key, part):
    cached = cache_base(key)
    return widen(cached).astype(jnp.bfloat16)


def draw_new_keys(key, part):
    return widen(fresh_base(key)).astype(jnp.bfloat16)


def draw_cache_values(key, part):
    key = jax.random.fold_in(key, 7)
    drawn = jnp.clip(jax.random.normal(key, (REQUESTS, CTX, KVH, HD), jnp.float32), -5.0, 5.0)
    return widen(drawn).astype(jnp.bfloat16)


def draw_new_values(key, part):
    key = jax.random.fold_in(key, 8)
    drawn = jnp.clip(jax.random.normal(key, (STEPS, REQUESTS, KVH, HD), jnp.float32), -5.0, 5.0)
    return widen(drawn).astype(jnp.bfloat16)


def draw_queries(key, part):
    own_keys = jnp.repeat(fresh_base(key), HQ // KVH, axis=2)
    key = jax.random.fold_in(key, 9)
    noise = jnp.clip(jax.random.normal(key, (STEPS, REQUESTS, HQ, HD), jnp.float32), -4.0, 4.0)
    mixed = noise + 0.25 * own_keys
    return mixed.reshape(STEPS, REQUESTS, HQ * HD).astype(jnp.bfloat16)


def with_ends(values, stream_key, smallest, largest):
    longest = values.shape.index(max(values.shape))
    spots = []
    for shift in (0, 1):
        where = [jax.random.randint(jax.random.fold_in(stream_key, axis), (), 0, length) for axis, length in enumerate(values.shape)]
        where[longest] = (where[longest] + shift) % values.shape[longest]
        spots.append(tuple(where))
    return values.at[spots[0]].set(smallest).at[spots[1]].set(largest)


def shard_levels(key, dims, cuts, low, largest):
    level = 1.0
    for position, shards_of in cuts:
        heights = jax.random.uniform(jax.random.fold_in(jax.random.fold_in(key, 6), position), (shards_of,), jnp.float32, low / len(cuts), largest / len(cuts))
        level = level * jnp.repeat(jnp.exp(heights), dims[position] // shards_of).reshape((-1,) + (1,) * (len(dims) - 1 - position))
    return level


def normal_values(own_key, shape, width, most, cuts=(), held_as=jnp.bfloat16):
    entries = jax.random.normal(own_key, shape, jnp.float32) * width
    if len(cuts) > 0:
        entries = shard_levels(own_key, shape, cuts, -0.22, 0.18) * entries
    return jnp.clip(entries, min=-most, max=most).astype(held_as)


def setup_inputs(seed: int = 0) -> dict:
    splits = jax.random.split(jax.random.key(seed), 15)
    return {
        "queries": draw_queries(jax.random.fold_in(splits[14], 71), 0),
        "cache_keys": draw_cache_keys(jax.random.fold_in(splits[14], 71), 0),
        "cache_values": draw_cache_values(jax.random.fold_in(splits[14], 71), 0),
        "new_keys": draw_new_keys(jax.random.fold_in(splits[14], 71), 0),
        "new_values": draw_new_values(jax.random.fold_in(splits[14], 71), 0),
        "lengths": draw_lengths(jax.random.fold_in(splits[14], 71), 0),
        "admitted": with_ends((jax.random.randint(splits[6], (STEPS, REQUESTS), 0, 4) < 3).astype(jnp.int32), jax.random.fold_in(splits[6], 1), 0, 1),
        "request_tenant": draw_request_tenant(jax.random.fold_in(splits[14], 71), 0),
        "tenant_adapter": draw_tenant_adapter(jax.random.fold_in(splits[14], 71), 0),
        "adapter_slot": draw_adapter_slot(jax.random.fold_in(splits[14], 71), 0),
        "tenant_tokens": with_ends(jax.random.randint(splits[10], (TENANTS,), 0, 4 * CTX), jax.random.fold_in(splits[10], 1), 0, (4 * CTX) - 1).astype(jnp.int32),
        "out_weight": normal_values(splits[11], (HQ * HD, D), (HQ * HD) ** -0.5, 0.0625, ((0, 16),)),
        "adapter_down_factor": normal_values(splits[12], (ADAPTERS, RANK, HQ * HD), (HQ * HD) ** -0.5, 0.0625, ((0, 16), (2, 16))),
        "adapter_up_factor": normal_values(splits[13], (ADAPTERS, RANK, D), RANK ** -0.5, 0.75, ((0, 16), (2, 16))),
    }


adapter_scale = 2.0


def rounded(value):
    return lax.optimization_barrier(value.astype(jnp.bfloat16)).astype(jnp.float32)


def adapter_term_rows(attended_output, request_adapter_slot, adapter_down_factor, adapter_up_factor):
    def single(item):
        attended_row, slot_index = item
        first_factor = lax.dynamic_index_in_dim(adapter_down_factor, slot_index, 0, keepdims=False).astype(jnp.float32)
        second_factor = lax.dynamic_index_in_dim(adapter_up_factor, slot_index, 0, keepdims=False).astype(jnp.float32)
        low_rank = rounded(jnp.dot(first_factor, attended_row.astype(jnp.float32)))
        return jnp.dot(low_rank, second_factor)
    return lax.map(single, (attended_output, request_adapter_slot))


def reference(queries, cache_keys, cache_values, new_keys, new_values, lengths, admitted, request_tenant, tenant_adapter, adapter_slot, tenant_tokens, out_weight, adapter_down_factor, adapter_up_factor):
    score_scale = HD ** -0.5
    cached_keys = cache_keys.astype(jnp.float32)
    cached_values = cache_values.astype(jnp.float32)
    fresh_keys = new_keys.astype(jnp.float32)
    fresh_values = new_values.astype(jnp.float32)
    positions = jnp.arange(CTX, dtype=jnp.int32)
    cache_mask = positions[None, :] < lengths[:, None]
    request_adapter_slot = jnp.take(adapter_slot, jnp.take(tenant_adapter, request_tenant)).astype(jnp.int32)
    counters = tenant_tokens
    served_rows = []
    results = []
    for step_index in range(STEPS):
        served = (admitted[step_index] == 1) & (jnp.take(counters, request_tenant) < LIMIT)
        served_rows.append(served)
        query_rows = queries[step_index].astype(jnp.float32).reshape(REQUESTS, KV_SLOTS, HEADS_DEV, HD)
        old_scores = jnp.einsum("rchd,rpcd->rchp", query_rows, cached_keys) * score_scale
        old_scores = jnp.where(cache_mask[:, None, None, :], old_scores, -jnp.inf)
        visible = jnp.stack([served_rows[other] if other < step_index else jnp.full((REQUESTS,), other == step_index) for other in range(STEPS)], axis=1)
        new_scores = jnp.einsum("rchd,jrcd->rchj", query_rows, fresh_keys) * score_scale
        new_scores = jnp.where(visible[:, None, None, :], new_scores, -jnp.inf)
        row_max = jnp.maximum(jnp.max(old_scores, axis=-1), jnp.max(new_scores, axis=-1))
        old_exp = jnp.exp(old_scores - row_max[..., None])
        new_exp = jnp.exp(new_scores - row_max[..., None])
        denominator = jnp.sum(old_exp, axis=-1) + jnp.sum(new_exp, axis=-1)
        old_weights = rounded(old_exp / denominator[..., None])
        new_weights = rounded(new_exp / denominator[..., None])
        attended_output = jnp.einsum("rchp,rpcd->rchd", old_weights, cached_values) + jnp.einsum("rchj,jrcd->rchd", new_weights, fresh_values)
        attended_output = attended_output.reshape(REQUESTS, HQ * HD).astype(jnp.bfloat16)
        base_projection_term = jnp.dot(attended_output, out_weight, preferred_element_type=jnp.float32)
        adapter_correction = adapter_term_rows(attended_output, request_adapter_slot, adapter_down_factor, adapter_up_factor)
        combined_output = base_projection_term + adapter_scale * adapter_correction
        results.append(jnp.where(served[:, None], combined_output, 0.0).astype(jnp.bfloat16))
        charge = jnp.where(served, lengths + step_index + 1, 0).astype(jnp.int32)
        counters = (counters + jax.ops.segment_sum(charge, request_tenant, num_segments=TENANTS)).astype(jnp.int32)
    return jnp.stack(results)
```

```python
import functools

import jax
import jax.numpy as jnp
from jax import lax
from jax.experimental import pallas as pl
from jax.experimental.pallas import tpu as pltpu
from jax.sharding import Mesh
from jax.sharding import PartitionSpec as P

adapter_scale = 2.0
capacity = 2
lanes = 128
f32 = jnp.float32
bf16 = jnp.bfloat16
VMEM = pl.BlockSpec(memory_space=pltpu.VMEM)
SMEM = pl.BlockSpec(memory_space=pltpu.SMEM)
HBM = pl.BlockSpec(memory_space=pl.ANY)


def iota(shape, axis):
    return lax.broadcasted_iota(jnp.int32, shape, axis)


def dot(a, b):
    return jnp.dot(a, b, preferred_element_type=f32)


def dot_t(a, b):
    return lax.dot_general(a, b, (((1,), (1,)), ((), ())), preferred_element_type=f32)


def call(kernel, out_shape, in_specs, out_specs, flops, moved, scratch=(), limit=48 << 20):
    return pl.pallas_call(
        kernel,
        out_shape=out_shape,
        in_specs=in_specs,
        out_specs=out_specs,
        scratch_shapes=list(scratch),
        cost_estimate=pl.CostEstimate(flops=flops, bytes_accessed=moved, transcendentals=0),
        compiler_params=pltpu.CompilerParams(vmem_limit_bytes=limit),
    )


def score_kernel(
    steps,
    requests,
    heads,
    adapters_held,
    tenant_ref,
    length_ref,
    tenant_adapter_ref,
    adapter_slot_ref,
    query_ref,
    key_ref,
    new_key_ref,
    exp_ref,
    stat_ref,
    new_score_ref,
    flat_ref,
    held_ref,
    back_ref,
    seen,
):
    rows = steps * heads
    total = requests * rows
    width = key_ref.shape[2]
    context = key_ref.shape[1]
    scale = width ** (-0.5)
    for index in range(seen.shape[0]):
        seen[index] = 0
    flat_rows = jnp.zeros((steps * requests, 1), jnp.int32)
    place = iota((steps * requests, 1), 0)
    for r in range(requests):
        slot = adapter_slot_ref[tenant_adapter_ref[tenant_ref[r]]]
        holder = slot // adapters_held
        position = seen[holder]
        seen[holder] = position + 1
        flat = holder * capacity + position
        flat_ref[r] = flat
        held_ref[r] = slot - holder * adapters_held
        flat_rows = jnp.where(place % requests == r, flat, flat_rows)
    flat_rows = flat_rows * steps + place // requests
    back_ref[...] = (flat_rows == iota(back_ref.shape, 1)).astype(f32).astype(bf16)

    by_head = jnp.concatenate(
        [query_ref[:, h * width : (h + 1) * width] for h in range(heads)], axis=0
    )
    row = iota((total, total), 0)
    wanted = (row % heads) * (steps * requests) + ((row // heads) % steps) * requests + row // rows
    order = (wanted == iota((total, total), 1)).astype(f32).astype(bf16)
    by_request = dot(order, by_head).astype(bf16)
    new_score_ref[...] = dot_t(by_request, new_key_ref[...]) * scale
    position = iota((rows, context), 1)
    for r in range(requests):
        block = pl.ds(r * rows, rows)
        scores = dot_t(by_request[r * rows : (r + 1) * rows], key_ref[r]) * scale
        scores = jnp.where(position < length_ref[r], scores, -jnp.inf)
        top = jnp.max(scores, axis=1, keepdims=True)
        weight = jnp.exp(scores - top)
        exp_ref[block, :] = weight
        mass = jnp.sum(weight, axis=1, keepdims=True)
        stat_ref[block, :] = jnp.where(iota((rows, lanes), 1) == 0, top, mass)


def attend_kernel(
    steps,
    requests,
    heads,
    threshold,
    tenant_ref,
    token_ref,
    admitted_ref,
    flat_ref,
    held_ref,
    shared_ref,
    exp_ref,
    stat_ref,
    new_score_ref,
    value_ref,
    new_value_ref,
    home_ref,
    send_ref,
    attended,
):
    rows = steps * heads
    total = requests * rows
    width = value_ref.shape[2]
    tenants = shared_ref[:, 0, :]
    lengths = shared_ref[:, 1, :]
    charges = [
        jnp.where(shared_ref[:, 2 + s, :] == 1, lengths + (s + 1), 0).astype(f32)
        for s in range(steps - 1)
    ]
    step_of_row = iota((rows, 1), 0) // heads
    column = iota((rows, steps * requests), 1)
    column_step = column // requests
    for r in range(requests):
        block = pl.ds(r * rows, rows)
        same = tenants == tenant_ref[r]
        count = jnp.full((1, 1), token_ref[tenant_ref[r]], jnp.int32)
        served = []
        for s in range(steps):
            open_now = (count < threshold).astype(jnp.int32)
            served.append(open_now * (admitted_ref[s, r] == 1).astype(jnp.int32))
            if s + 1 < steps:
                charge = jnp.sum(jnp.where(same, charges[s], 0.0), axis=(0, 1), keepdims=True)
                count = count + open_now * charge.astype(jnp.int32)
        visible_step = jnp.zeros((rows, steps * requests), jnp.int32)
        served_row = jnp.zeros((rows, 1), f32)
        for s in range(steps):
            visible_step = jnp.where(column_step == s, served[s], visible_step)
            served_row = jnp.where(step_of_row == s, served[s].astype(f32), served_row)
        visible = (column_step == step_of_row) | (
            (column_step < step_of_row) & (visible_step == 1)
        )
        visible = visible & (column % requests == r)
        new_scores = jnp.where(visible, new_score_ref[block, :], -jnp.inf)
        old_top = stat_ref[block, 0:1]
        top = jnp.maximum(old_top, jnp.max(new_scores, axis=1, keepdims=True))
        shrink = jnp.exp(old_top - top)
        new_exp = jnp.exp(new_scores - top)
        mass = stat_ref[block, 1:2] * shrink + jnp.sum(new_exp, axis=1, keepdims=True)
        inverse = 1.0 / mass
        old_weights = (exp_ref[block, :] * (shrink * inverse)).astype(bf16)
        new_weights = (new_exp * inverse).astype(bf16)
        gathered = dot(old_weights, value_ref[r]) + dot(new_weights, new_value_ref[...])
        attended[block, :] = (gathered * served_row).astype(bf16)
    row = iota((total, total), 0)
    pairs = steps * requests
    wanted = (row % requests) * rows + ((row // requests) % steps) * heads + row // pairs
    order = (wanted == iota((total, total), 1)).astype(f32).astype(bf16)
    by_head = dot(order, attended[...]).astype(bf16)
    for h in range(heads):
        home_ref[:, h * width : (h + 1) * width] = by_head[h * pairs : (h + 1) * pairs]
    lane = iota((1, pairs), 1)
    flat = jnp.zeros((1, pairs), jnp.int32)
    place = iota((pairs, lanes), 0) % requests
    held = jnp.zeros((pairs, lanes), f32)
    for r in range(requests):
        flat = jnp.where(lane % requests == r, flat_ref[r], flat)
        held = jnp.where(place == r, held_ref[r].astype(f32), held)
    flat = flat * steps + lane // requests
    pick = (iota((send_ref.shape[0], pairs), 0) == flat).astype(f32).astype(bf16)
    features = heads * width
    send_ref[:, 0:features] = dot(pick, home_ref[...]).astype(bf16)
    send_ref[:, features:] = dot(pick, held.astype(bf16)).astype(bf16)


def project_kernel(flip, rows_ref, weight_ref, out_ref, blocks, sems):
    parts, _, width = out_ref.shape
    core = lax.axis_index("core")
    mine = core if flip == 0 else 1 - core
    copies = []
    for part in range(parts):
        start = pl.multiple_of((2 * part + mine) * width, width)
        copy = pltpu.make_async_copy(
            weight_ref.at[:, pl.ds(start, width)], blocks.at[part], sems.at[part]
        )
        copy.start()
        copies.append(copy)
    for part in range(parts):
        copies[part].wait()
        out_ref[part] = dot(rows_ref[...], blocks[part]).astype(out_ref.dtype)


def low_kernel(got_ref, held_ref, down_ref, low_ref):
    rank = down_ref.shape[1]
    every = down_ref.shape[0] * rank
    features = down_ref.shape[2]
    product = dot_t(got_ref[...], down_ref[...].reshape(every, features))
    owner = (iota(product.shape, 1) // rank).astype(f32)
    product = jnp.where(owner == held_ref[:, 0:1].astype(f32), product, 0.0)
    folded = product[:, 0:lanes]
    for start in range(lanes, every, lanes):
        folded = folded + product[:, start : start + lanes]
    folded = folded + pltpu.roll(folded, rank, 1)
    half = folded.shape[0] // 2
    first = iota((half, lanes), 1) < rank
    low_ref[...] = jnp.where(first, folded[0:half], folded[half:])


def up_kernel(parts_ref, held_ref, up_ref, out_ref):
    rank = up_ref.shape[1]
    every = up_ref.shape[0] * rank
    low = parts_ref[0].astype(f32)
    for part in range(1, parts_ref.shape[0]):
        low = low + parts_ref[part].astype(f32)
    other = pltpu.roll(low, rank, 1)
    first = iota(low.shape, 1) < rank
    low = jnp.concatenate(
        [jnp.where(first, low, other), jnp.where(first, other, low)], axis=0
    )
    wide = jnp.concatenate([low] * (every // lanes), axis=1)
    owner = (iota(wide.shape, 1) // rank).astype(f32)
    wide = jnp.where(owner == held_ref[:, 0:1].astype(f32), wide, 0.0).astype(bf16)
    out_ref[...] = dot(wide, up_ref[...].reshape(every, up_ref.shape[2])).astype(bf16)


def finish_kernel(base_ref, back_ref, term_ref, out_ref):
    total = base_ref[0].astype(f32)
    for part in range(1, base_ref.shape[0]):
        total = total + base_ref[part].astype(f32)
    term = dot(back_ref[...], term_ref[...])
    out_ref[...] = (total + adapter_scale * term).astype(bf16)


def per_device(
    queries,
    cache_keys,
    cache_values,
    new_keys,
    new_values,
    lengths,
    admitted,
    request_tenant,
    tenant_adapter,
    adapter_slot,
    tenant_tokens,
    out_weight,
    adapter_down_factor,
    adapter_up_factor,
):
    holders = lax.axis_size("batch")
    parts = lax.axis_size("z")
    steps, requests, features = queries.shape
    context, width = cache_keys.shape[1], cache_keys.shape[3]
    heads = features // width
    rows = steps * heads
    total = requests * rows
    pairs = steps * requests
    adapters_held, rank, _ = adapter_down_factor.shape
    every = adapters_held * rank
    threshold = 3 * context
    slots = holders * capacity * steps
    shape = jax.ShapeDtypeStruct

    shared = jnp.concatenate([request_tenant[None], lengths[None], admitted], axis=0)
    shared = jnp.broadcast_to(shared[None], (holders,) + shared.shape)
    shared = lax.all_to_all(shared, "batch", split_axis=0, concat_axis=0, tiled=True)

    old_exp, stats, new_scores, flat, held, back = call(
        functools.partial(score_kernel, steps, requests, heads, adapters_held),
        (
            shape((total, context), f32),
            shape((total, lanes), f32),
            shape((total, pairs), f32),
            shape((requests,), jnp.int32),
            shape((requests,), jnp.int32),
            shape((pairs, slots), bf16),
        ),
        [SMEM, SMEM, SMEM, SMEM, VMEM, VMEM, VMEM],
        (VMEM, VMEM, VMEM, SMEM, SMEM, VMEM),
        2 * total * context * width,
        3 * cache_keys.size,
        [pltpu.SMEM((holders,), jnp.int32)],
    )(
        request_tenant,
        lengths,
        tenant_adapter,
        adapter_slot,
        queries.reshape(pairs, features),
        cache_keys.reshape(requests, context, width),
        new_keys.reshape(pairs, width),
    )
    home, send = call(
        functools.partial(attend_kernel, steps, requests, heads, threshold),
        (shape((pairs, features), bf16), shape((slots, features + lanes), bf16)),
        [SMEM] * 5 + [VMEM] * 6,
        (VMEM, VMEM),
        2 * total * context * width,
        3 * cache_keys.size,
        [pltpu.VMEM((total, width), bf16)],
    )(
        request_tenant,
        tenant_tokens,
        admitted,
        flat,
        held,
        shared,
        old_exp,
        stats,
        new_scores,
        cache_values.reshape(requests, context, width),
        new_values.reshape(pairs, width),
    )
    got = lax.all_to_all(send, "batch", split_axis=0, concat_axis=0, tiled=True)

    def project(flip, dtype):
        return call(
            functools.partial(project_kernel, flip),
            shape((parts, pairs, features), dtype),
            [VMEM, HBM],
            VMEM,
            pairs * out_weight.size,
            out_weight.size,
            [
                pltpu.VMEM((parts, features, features), bf16),
                pltpu.SemaphoreType.DMA((parts,)),
            ],
        )(home, out_weight)

    swap = [(0, 1), (1, 0)]
    theirs = lax.ppermute(project(1, bf16), "core", swap)
    ours = project(0, f32)
    base = (ours + theirs.astype(f32)).astype(bf16)

    rows_got = got[:, 0:features]
    held_got = got[:, features:]
    low = call(
        low_kernel,
        shape((slots // 2, lanes), f32),
        [VMEM] * 3,
        VMEM,
        2 * slots * features * every,
        4 * slots * features,
    )(rows_got, held_got, adapter_down_factor)
    low = (low + lax.ppermute(low, "core", swap)).astype(bf16)
    low = jnp.broadcast_to(low[None], (parts,) + low.shape)
    low = lax.all_to_all(low, "z", split_axis=0, concat_axis=0, tiled=True)
    base = lax.all_to_all(base, "z", split_axis=0, concat_axis=0, tiled=True)
    term = call(
        up_kernel,
        shape((slots, features), bf16),
        [VMEM] * 3,
        VMEM,
        2 * slots * features * every,
        4 * slots * features,
    )(low, held_got, adapter_up_factor)
    term = lax.all_to_all(term, "batch", split_axis=0, concat_axis=0, tiled=True)
    out = call(
        finish_kernel,
        shape((pairs, features), bf16),
        [VMEM] * 3,
        VMEM,
        2 * pairs * slots * features,
        4 * base.size,
    )(base, back, term)
    return out.reshape(steps, requests, features)


def solution(mesh):
    batch, tensor = mesh.shape["batch"], mesh.shape["tensor"]
    split = Mesh(mesh.devices.reshape(batch, tensor // 2, 2), ("batch", "z", "core"))
    tensor_axes = ("z", "core")
    placed = (
        P(None, "batch", tensor_axes),
        P("batch", None, tensor_axes, None),
        P("batch", None, tensor_axes, None),
        P(None, "batch", tensor_axes, None),
        P(None, "batch", tensor_axes, None),
        P("batch"),
        P(None, "batch"),
        P("batch"),
        P(),
        P(),
        P(),
        P(tensor_axes, None),
        P("batch", None, tensor_axes),
        P("batch", None, tensor_axes),
    )
    return jax.shard_map(
        per_device,
        mesh=split,
        in_specs=placed,
        out_specs=P(None, "batch", tensor_axes),
        check_vma=False,
    )
```

```python
import functools

import jax
import jax.numpy as jnp
from jax import lax
from jax.experimental import pallas as pl
from jax.experimental.pallas import tpu as pltpu
from jax.sharding import Mesh
from jax.sharding import PartitionSpec as P

adapter_scale = 2.0
capacity = 2
lanes = 128
f32 = jnp.float32
bf16 = jnp.bfloat16
VMEM = pl.BlockSpec(memory_space=pltpu.VMEM)
SMEM = pl.BlockSpec(memory_space=pltpu.SMEM)
HBM = pl.BlockSpec(memory_space=pltpu.HBM)


def in_hbm(array):
    return pltpu.with_memory_space_constraint(array, pltpu.HBM)


def in_vmem(array):
    return pltpu.with_memory_space_constraint(array, pltpu.VMEM)


def iota(shape, axis):
    return lax.broadcasted_iota(jnp.int32, shape, axis)


def dot(a, b):
    return jnp.dot(a, b, preferred_element_type=f32)


def dot_t(a, b):
    return lax.dot_general(a, b, (((1,), (1,)), ((), ())), preferred_element_type=f32)


def call(kernel, out_shape, in_specs, out_specs, flops, moved, scratch=(), limit=16 << 20):
    return pl.pallas_call(
        kernel,
        out_shape=out_shape,
        in_specs=in_specs,
        out_specs=out_specs,
        scratch_shapes=list(scratch),
        cost_estimate=pl.CostEstimate(flops=flops, bytes_accessed=moved, transcendentals=0),
        compiler_params=pltpu.CompilerParams(vmem_limit_bytes=limit),
    )


def fetch_all(pairs, sems):
    copies = []
    for index, (source, target) in enumerate(pairs):
        copy = pltpu.make_async_copy(source, target, sems.at[index])
        copy.start()
        copies.append(copy)
    return copies


def one_hot(wanted, shape):
    return (wanted == iota(shape, 1)).astype(f32).astype(bf16)


def attend_kernel(
    steps,
    requests,
    heads,
    adapters_held,
    tenant_in,
    length_in,
    admitted_in,
    tenant_adapter_in,
    adapter_slot_in,
    token_in,
    query_in,
    key_in,
    value_in,
    new_key_in,
    new_value_in,
    weight_in,
    home_ref,
    send_ref,
    back_ref,
    weight_ref,
    tenant_ref,
    length_ref,
    admitted_ref,
    tenant_adapter_ref,
    adapter_slot_ref,
    token_ref,
    seen,
    query_ref,
    key_ref,
    value_ref,
    new_key_ref,
    new_value_ref,
    attended,
    own_exp,
    masses,
    sems,
):
    rows = steps * heads
    total = requests * rows
    pairs = steps * requests
    width = key_ref.shape[2]
    context = key_ref.shape[1]
    features = heads * width
    scale = width ** (-0.5)
    copies = fetch_all(
        [
            (tenant_in, tenant_ref),
            (length_in, length_ref),
            (admitted_in, admitted_ref),
            (tenant_adapter_in, tenant_adapter_ref),
            (adapter_slot_in, adapter_slot_ref),
            (token_in, token_ref),
            (query_in, query_ref),
            (new_key_in, new_key_ref),
            (new_value_in, new_value_ref),
            (key_in, key_ref),
            (value_in, value_ref),
            (weight_in, weight_ref),
        ],
        sems,
    )
    for index in range(seen.shape[0]):
        seen[index] = 0
    for copy in copies[:9]:
        copy.wait()

    me = lax.axis_index("batch")
    lane = iota((1, lanes), 1)
    place = iota((pairs, 1), 0)
    lane_of_pair = iota((1, pairs), 1)
    shared_row = iota((8, 2 * lanes), 0)
    shared_lane = iota((8, 2 * lanes), 1)
    flat_rows = jnp.zeros((pairs, 1), jnp.int32)
    flat_lanes = jnp.zeros((1, pairs), jnp.int32)
    scalars = jnp.zeros((pairs, lanes), f32)
    shared = jnp.zeros((8, 2 * lanes), f32)
    first_scalar = 3 * heads * (steps - 1)
    for r in range(requests):
        tenant = tenant_ref[r]
        tokens = token_ref[tenant]
        slot = adapter_slot_ref[tenant_adapter_ref[tenant]]
        holder = slot // adapters_held
        position = seen[holder]
        seen[holder] = position + 1
        flat = (holder * capacity + position) * steps
        flat_rows = jnp.where(place // steps == r, flat, flat_rows)
        flat_lanes = jnp.where(lane_of_pair // steps == r, flat, flat_lanes)
        tenant_parts = [tenant // 16, tenant % 16]
        admits = [admitted_ref[s, r] for s in range(steps)]
        own = [slot - holder * adapters_held] + tenant_parts + [tokens // 32, tokens % 32] + admits
        line = jnp.zeros((1, lanes), jnp.int32)
        for index, value in enumerate(own):
            line = jnp.where(lane == first_scalar + index, value, line)
        scalars = jnp.where(place // steps == r, line.astype(f32), scalars)
        column = jnp.zeros((8, 2 * lanes), jnp.int32)
        for index, value in enumerate(tenant_parts + [length_ref[r]] + admits):
            column = jnp.where(shared_row == index, value, column)
        shared = jnp.where(shared_lane == me * requests + r, column.astype(f32), shared)
    flat_rows = flat_rows + place % steps
    flat_lanes = flat_lanes + lane_of_pair % steps
    back_ref[...] = one_hot(flat_rows, back_ref.shape)

    by_head = jnp.concatenate(
        [query_ref[:, h * width : (h + 1) * width] for h in range(heads)], axis=0
    )
    row = iota((total, total), 0)
    wanted = (row % heads) * pairs + ((row // heads) % steps) * requests + row // rows
    by_request = dot(one_hot(wanted, (total, total)), by_head).astype(bf16)
    new_scores = dot_t(by_request, new_key_ref[...]) * scale
    row = iota((total, 1), 0)
    new_column = iota((total, pairs), 1)
    by_step = [
        jnp.sum(
            jnp.where(new_column == j * requests + row // rows, new_scores, 0.0),
            axis=1,
            keepdims=True,
        )
        for j in range(steps)
    ]
    step_of_row = (row // heads) % steps
    own_score = by_step[0]
    for s in range(1, steps):
        own_score = jnp.where(step_of_row == s, by_step[s], own_score)
    own_place = new_column == step_of_row * requests + row // rows
    position = iota((rows, context), 1)
    copies[9].wait()
    copies[10].wait()
    for r in range(requests):
        block = pl.ds(r * rows, rows)
        scores = dot_t(by_request[r * rows : (r + 1) * rows], key_ref[r]) * scale
        scores = jnp.where(position < length_ref[r], scores, -jnp.inf)
        own = own_score[r * rows : (r + 1) * rows]
        top = jnp.maximum(jnp.max(scores, axis=1, keepdims=True), own)
        weight = jnp.exp(scores - top)
        own_weight = jnp.exp(own - top)
        mass = jnp.sum(weight, axis=1, keepdims=True) + own_weight
        inverse = 1.0 / mass
        attended[block, :] = dot((weight * inverse).astype(bf16), value_ref[r])
        own_exp[block, :] = jnp.broadcast_to(own_weight * inverse, (rows, lanes))
        masses[block, :] = jnp.broadcast_to(top + jnp.log(mass), (rows, lanes))
    own_weights = jnp.where(own_place, own_exp[:, 0:pairs], 0.0).astype(bf16)
    result = (attended[...] + dot(own_weights, new_value_ref[...])).astype(bf16)

    row = iota((total, total), 0)
    wanted = (row % pairs) * heads + row // pairs
    by_head = dot(one_hot(wanted, (total, total)), result).astype(bf16)
    for h in range(heads):
        home_ref[:, h * width : (h + 1) * width] = by_head[h * pairs : (h + 1) * pairs]
    place = iota((pairs, 1), 0)
    wanted = (place % steps) * requests + place // steps
    values = dot(one_hot(wanted, (pairs, pairs)), new_value_ref[...])
    home_ref[:, features : features + width] = values.astype(bf16)
    row = iota((total, 1), 0)
    lane = iota((total, lanes), 1)
    log_mass = masses[:, 0:1]
    pieces = jnp.zeros((total, lanes), f32)
    for j in range(steps - 1):
        rest = by_step[j] - log_mass
        for piece in range(3):
            part = rest.astype(bf16).astype(f32)
            rest = rest - part
            target = (piece * (steps - 1) + j) * heads + row % heads
            pieces = jnp.where(lane == target, part, pieces)
    gather = (iota((pairs, total), 1) // heads == iota((pairs, total), 0)).astype(f32).astype(bf16)
    scalars = scalars + dot(gather, pieces.astype(bf16))
    home_ref[:, features + width :] = scalars.astype(bf16)
    slots = send_ref.shape[0]
    pick = (iota((slots, pairs), 0) == flat_lanes).astype(f32).astype(bf16)
    sent = features + width + lanes
    send_ref[:, 0:sent] = dot(pick, home_ref[...]).astype(bf16)
    spread = (iota((slots, 8), 0) % 8 == iota((slots, 8), 1)).astype(f32).astype(bf16)
    send_ref[:, sent:] = dot(spread, shared.astype(bf16)).astype(bf16)
    copies[11].wait()


def combine_kernel(
    steps,
    heads,
    width,
    threshold,
    got_ref,
    home_ref,
    down_ref,
    weight_ref,
    low_ref,
    theirs_ref,
    ours_ref,
    rows_ref,
    final_ref,
):
    slots, pairs = got_ref.shape[0], home_ref.shape[0]
    features = heads * width
    sent = features + width + lanes
    count = slots + pairs
    shared = got_ref[0:8, sent:].astype(f32)
    for start in range(8, slots, 8):
        shared = shared + got_ref[start : start + 8, sent:].astype(f32)
    tenants = shared[0:1] * 16.0 + shared[1:2]
    charge_rows = []
    for s in range(steps - 1):
        charge = shared[2:3] + (s + 1.0)
        upper = jnp.floor(charge * (1.0 / 16.0))
        admitted = shared[3 + s : 4 + s]
        charge_rows += [upper * admitted, (charge - upper * 16.0) * admitted]
    charge_rows += [jnp.zeros_like(tenants)] * (8 - len(charge_rows))
    charges = jnp.concatenate(charge_rows, axis=0).astype(bf16)

    block = features + width
    scalars = jnp.concatenate(
        [got_ref[:, block:sent].astype(f32), home_ref[:, block:sent].astype(f32)], axis=0
    )
    first = 3 * heads * (steps - 1)
    tenant = scalars[:, first + 1 : first + 2] * 16.0 + scalars[:, first + 2 : first + 3]
    tokens = scalars[:, first + 3 : first + 4] * 32.0 + scalars[:, first + 4 : first + 5]
    same = (tenant == tenants).astype(f32).astype(bf16)
    grows = dot_t(same, charges)
    step_of_row = iota((count, 1), 0) % steps
    served_now = jnp.zeros((count, 1), f32)
    served = []
    for s in range(steps):
        open_now = (tokens < threshold).astype(f32)
        flag = open_now * scalars[:, first + 5 + s : first + 6 + s]
        served.append(flag)
        served_now = jnp.where(step_of_row == s, flag, served_now)
        if s + 1 < steps:
            grow = grows[:, 2 * s : 2 * s + 1] * 16.0 + grows[:, 2 * s + 1 : 2 * s + 2]
            tokens = tokens + open_now * grow

    span = heads * (steps - 1)
    logs = scalars[:, 0:span] + scalars[:, span : 2 * span] + scalars[:, 2 * span : 3 * span]
    shown = [(served[j] > 0.5) & (step_of_row > j) for j in range(steps - 1)]
    by_step = [
        jnp.where(shown[j], logs[:, j * heads : (j + 1) * heads], -jnp.inf)
        for j in range(steps - 1)
    ]
    top = jnp.zeros((count, heads), f32)
    for j in range(steps - 1):
        top = jnp.maximum(top, by_step[j])
    old = jnp.exp(-top)
    new = [jnp.exp(by_step[j] - top) for j in range(steps - 1)]
    mass = old
    for j in range(steps - 1):
        mass = mass + new[j]
    inverse = served_now / mass
    old = old * inverse
    new = [weight * inverse for weight in new]
    values = jnp.concatenate(
        [got_ref[:, features:block], home_ref[:, features:block]], axis=0
    )
    row = iota((count, 1), 0)
    new_values = [
        dot(one_hot(row - row % steps + j, (count, count)), values) for j in range(steps - 1)
    ]
    for h in range(heads):
        part = slice(h * width, (h + 1) * width)
        rows = jnp.concatenate([got_ref[:, part], home_ref[:, part]], axis=0).astype(f32)
        rows = rows * old[:, h : h + 1]
        for j in range(steps - 1):
            rows = rows + new_values[j] * new[j][:, h : h + 1]
        rows = rows.astype(bf16)
        rows_ref[:, part] = rows[0:slots]
        final_ref[:, part] = rows[slots:]

    rank = down_ref.shape[1]
    every = down_ref.shape[0] * rank
    product = dot_t(rows_ref[...], down_ref[...].reshape(every, features))
    owner = (iota(product.shape, 1) // rank).astype(f32)
    product = jnp.where(owner == scalars[0:slots, first : first + 1], product, 0.0)
    folded = product[:, 0:lanes]
    for start in range(lanes, every, lanes):
        folded = folded + product[:, start : start + lanes]
    folded = folded + pltpu.roll(folded, rank, 1)
    half = slots // 2
    low_half = iota((half, lanes), 1) < rank
    low_ref[...] = jnp.where(low_half, folded[0:half], folded[half:])
    parts, _, size = ours_ref.shape
    core = lax.axis_index("core")
    here = lax.axis_index("z")
    for out_ref, column in ((theirs_ref, 1 - core), (ours_ref, core)):
        for part in range(parts):
            target = lax.rem(here + part, parts)
            start = pl.multiple_of((2 * target + column) * size, size)
            product = dot(final_ref[...], weight_ref[:, pl.ds(start, size)])
            out_ref[part] = product.astype(out_ref.dtype)


def spread_kernel(low_ref, low_other_ref, base_ref, low_out):
    low = (low_ref[...] + low_other_ref[...]).astype(bf16)
    for part in range(low_out.shape[0]):
        low_out[part] = low


def mix_kernel(ours_ref, theirs_ref, base_out):
    for part in range(base_out.shape[0]):
        base_out[part] = (ours_ref[part] + theirs_ref[part].astype(f32)).astype(bf16)


def hop_kernel(distance, own_ref, first_ref, second_ref, first_out, second_out):
    back = own_ref.shape[0] - distance
    first_out[...] = (first_ref[...].astype(f32) + own_ref[distance].astype(f32)).astype(bf16)
    second_out[...] = (second_ref[...].astype(f32) + own_ref[back].astype(f32)).astype(bf16)


def start_kernel(distance, own_ref, first_ref, first_out, second_out):
    back = own_ref.shape[0] - distance
    first_out[...] = (first_ref[...].astype(f32) + own_ref[distance].astype(f32)).astype(bf16)
    second_out[...] = own_ref[back]


def up_kernel(first_scalar, parts_ref, held_ref, up_ref, out_ref):
    rank = up_ref.shape[1]
    every = up_ref.shape[0] * rank
    low = parts_ref[0].astype(f32)
    for part in range(1, parts_ref.shape[0]):
        low = low + parts_ref[part].astype(f32)
    other = pltpu.roll(low, rank, 1)
    first = iota(low.shape, 1) < rank
    low = jnp.concatenate(
        [jnp.where(first, low, other), jnp.where(first, other, low)], axis=0
    )
    wide = jnp.concatenate([low] * (every // lanes), axis=1)
    owner = (iota(wide.shape, 1) // rank).astype(f32)
    held = held_ref[:, first_scalar : first_scalar + 1].astype(f32)
    wide = jnp.where(owner == held, wide, 0.0).astype(bf16)
    out_ref[...] = dot(wide, up_ref[...].reshape(every, up_ref.shape[2])).astype(bf16)


def finish_kernel(steps, own_ref, first_ref, second_ref, back_ref, term_ref, out_ref):
    pairs = out_ref.shape[0]
    total = own_ref[0].astype(f32) + first_ref[...].astype(f32) + second_ref[...].astype(f32)
    term = dot(back_ref[...], term_ref[...])
    rows = (total + adapter_scale * term).astype(bf16)
    place = iota((pairs, 1), 0)
    requests = pairs // steps
    wanted = (place % requests) * steps + place // requests
    out_ref[...] = dot(one_hot(wanted, (pairs, pairs)), rows).astype(bf16)


def per_device(
    queries,
    cache_keys,
    cache_values,
    new_keys,
    new_values,
    lengths,
    admitted,
    request_tenant,
    tenant_adapter,
    adapter_slot,
    tenant_tokens,
    out_weight,
    adapter_down_factor,
    adapter_up_factor,
):
    holders = lax.axis_size("batch")
    parts = lax.axis_size("z")
    steps, requests, features = queries.shape
    context, width = cache_keys.shape[1], cache_keys.shape[3]
    heads = features // width
    rows = steps * heads
    total = requests * rows
    pairs = steps * requests
    adapters_held, rank, _ = adapter_down_factor.shape
    every = adapters_held * rank
    threshold = float(3 * context)
    slots = holders * capacity * steps
    first_scalar = 3 * heads * (steps - 1)
    sent = features + width + lanes
    shape = jax.ShapeDtypeStruct

    home, send, back, weight = call(
        functools.partial(attend_kernel, steps, requests, heads, adapters_held),
        (
            shape((pairs, sent), bf16),
            shape((slots, sent + 2 * lanes), bf16),
            shape((pairs, slots), bf16),
            pltpu.VMEM(out_weight.shape, bf16),
        ),
        [HBM] * 12,
        (VMEM,) * 4,
        4 * total * context * width,
        4 * cache_keys.size,
        [
            pltpu.SMEM((requests,), jnp.int32),
            pltpu.SMEM((requests,), jnp.int32),
            pltpu.SMEM((steps, requests), jnp.int32),
            pltpu.SMEM(tenant_adapter.shape, jnp.int32),
            pltpu.SMEM(adapter_slot.shape, jnp.int32),
            pltpu.SMEM(tenant_tokens.shape, jnp.int32),
            pltpu.SMEM((holders,), jnp.int32),
            pltpu.VMEM((pairs, features), bf16),
            pltpu.VMEM((requests, context, width), bf16),
            pltpu.VMEM((requests, context, width), bf16),
            pltpu.VMEM((pairs, width), bf16),
            pltpu.VMEM((pairs, width), bf16),
            pltpu.VMEM((total, width), f32),
            pltpu.VMEM((total, lanes), f32),
            pltpu.VMEM((total, lanes), f32),
            pltpu.SemaphoreType.DMA((12,)),
        ],
        40 << 20,
    )(
        *map(
            in_hbm,
            (
                request_tenant,
                lengths,
                admitted,
                tenant_adapter,
                adapter_slot,
                tenant_tokens,
                queries.reshape(pairs, features),
                cache_keys.reshape(requests, context, width),
                cache_values.reshape(requests, context, width),
                new_keys.reshape(pairs, width),
                new_values.reshape(pairs, width),
                out_weight,
            ),
        )
    )
    got = lax.all_to_all(send, "batch", split_axis=0, concat_axis=0, tiled=True)
    low, theirs, ours = call(
        functools.partial(combine_kernel, steps, heads, width, threshold),
        (
            shape((slots // 2, lanes), f32),
            shape((parts, pairs, features), bf16),
            shape((parts, pairs, features), f32),
        ),
        [VMEM] * 4,
        (VMEM,) * 3,
        2 * slots * features * every,
        out_weight.size,
        [pltpu.VMEM((slots, features), bf16), pltpu.VMEM((pairs, features), bf16)],
    )(got, home, adapter_down_factor, in_vmem(weight))
    swap = [(0, 1), (1, 0)]
    low_other = lax.ppermute(low, "core", swap)
    theirs = lax.ppermute(theirs, "core", swap)
    base = call(
        mix_kernel,
        shape((parts, pairs, features), bf16),
        [VMEM] * 2,
        VMEM,
        2 * ours.size,
        8 * ours.size,
    )(ours, theirs)
    low = call(
        spread_kernel,
        shape((parts, slots // 2, lanes), bf16),
        [VMEM, VMEM, HBM],
        VMEM,
        2 * low.size,
        24 * low.size,
    )(low, low_other, base)

    block = shape((pairs, features), bf16)
    ahead = [(i, (i + 1) % parts) for i in range(parts)]
    behind = [(i, (i - 1) % parts) for i in range(parts)]
    half = parts // 2
    forth = lax.ppermute(base[half], "z", ahead)
    low = lax.all_to_all(low, "z", split_axis=0, concat_axis=0, tiled=True)
    travelling = (forth,)
    for distance in range(half - 1, 0, -1):
        kernel = start_kernel if len(travelling) == 1 else hop_kernel
        forth, backward = call(
            functools.partial(kernel, distance),
            (block, block),
            [VMEM] * (1 + len(travelling)),
            (VMEM, VMEM),
            2 * block.size,
            12 * block.size,
        )(base, *travelling)
        travelling = (
            lax.ppermute(forth, "z", ahead),
            lax.ppermute(backward, "z", behind),
        )

    term = call(
        functools.partial(up_kernel, first_scalar),
        shape((slots, features), bf16),
        [VMEM] * 3,
        VMEM,
        2 * slots * features * every,
        4 * slots * features,
    )(low, got[:, features + width : sent], adapter_up_factor)
    term = lax.all_to_all(term, "batch", split_axis=0, concat_axis=0, tiled=True)
    out = call(
        functools.partial(finish_kernel, steps),
        block,
        [VMEM] * 5,
        VMEM,
        2 * pairs * slots * features,
        10 * block.size,
    )(base, *travelling, back, term)
    return out.reshape(steps, requests, features)


def solution(mesh):
    batch, tensor = mesh.shape["batch"], mesh.shape["tensor"]
    split = Mesh(mesh.devices.reshape(batch, tensor // 2, 2), ("batch", "z", "core"))
    tensor_axes = ("z", "core")
    placed = (
        P(None, "batch", tensor_axes),
        P("batch", None, tensor_axes, None),
        P("batch", None, tensor_axes, None),
        P(None, "batch", tensor_axes, None),
        P(None, "batch", tensor_axes, None),
        P("batch"),
        P(None, "batch"),
        P("batch"),
        P(),
        P(),
        P(),
        P(tensor_axes, None),
        P("batch", None, tensor_axes),
        P("batch", None, tensor_axes),
    )
    return jax.shard_map(
        per_device,
        mesh=split,
        in_specs=placed,
        out_specs=P(None, "batch", tensor_axes),
        check_vma=False,
    )
```

```python
import functools

import jax
import jax.numpy as jnp
from jax import lax
from jax.experimental import pallas as pl
from jax.experimental.pallas import tpu as pltpu
from jax.sharding import Mesh
from jax.sharding import PartitionSpec as P

adapter_scale = 2.0
capacity = 2
lanes = 128
f32 = jnp.float32
bf16 = jnp.bfloat16
VMEM = pl.BlockSpec(memory_space=pltpu.VMEM)
SMEM = pl.BlockSpec(memory_space=pltpu.SMEM)
HBM = pl.BlockSpec(memory_space=pltpu.HBM)


def in_hbm(array):
    return pltpu.with_memory_space_constraint(array, pltpu.HBM)


def in_vmem(array):
    return pltpu.with_memory_space_constraint(array, pltpu.VMEM)


def iota(shape, axis):
    return lax.broadcasted_iota(jnp.int32, shape, axis)


def dot(a, b):
    return jnp.dot(a, b, preferred_element_type=f32)


def dot_t(a, b):
    return lax.dot_general(a, b, (((1,), (1,)), ((), ())), preferred_element_type=f32)


def call(kernel, out_shape, in_specs, out_specs, flops, moved, scratch=(), limit=16 << 20):
    return pl.pallas_call(
        kernel,
        out_shape=out_shape,
        in_specs=in_specs,
        out_specs=out_specs,
        scratch_shapes=list(scratch),
        cost_estimate=pl.CostEstimate(flops=flops, bytes_accessed=moved, transcendentals=0),
        compiler_params=pltpu.CompilerParams(vmem_limit_bytes=limit),
    )


def fetch_all(pairs, sems):
    copies = []
    for index, (source, target) in enumerate(pairs):
        copy = pltpu.make_async_copy(source, target, sems.at[index])
        copy.start()
        copies.append(copy)
    return copies


def one_hot(wanted, shape):
    return (wanted == iota(shape, 1)).astype(f32).astype(bf16)


def attend_kernel(
    steps,
    requests,
    heads,
    adapters_held,
    tenant_in,
    length_in,
    admitted_in,
    tenant_adapter_in,
    adapter_slot_in,
    token_in,
    query_in,
    key_in,
    value_in,
    new_key_in,
    new_value_in,
    weight_in,
    home_ref,
    send_ref,
    back_ref,
    weight_ref,
    tenant_ref,
    length_ref,
    admitted_ref,
    tenant_adapter_ref,
    adapter_slot_ref,
    token_ref,
    seen,
    query_ref,
    key_ref,
    value_ref,
    new_key_ref,
    new_value_ref,
    attended,
    own_exp,
    masses,
    sems,
):
    rows = steps * heads
    total = requests * rows
    pairs = steps * requests
    width = key_ref.shape[2]
    context = key_ref.shape[1]
    features = heads * width
    scale = width ** (-0.5)
    copies = fetch_all(
        [
            (tenant_in, tenant_ref),
            (length_in, length_ref),
            (admitted_in, admitted_ref),
            (tenant_adapter_in, tenant_adapter_ref),
            (adapter_slot_in, adapter_slot_ref),
            (token_in, token_ref),
            (query_in, query_ref),
            (new_key_in, new_key_ref),
            (new_value_in, new_value_ref),
            (key_in, key_ref),
            (value_in, value_ref),
            (weight_in, weight_ref),
        ],
        sems,
    )
    for index in range(seen.shape[0]):
        seen[index] = 0
    for copy in copies[:9]:
        copy.wait()

    me = lax.axis_index("batch")
    lane = iota((1, lanes), 1)
    place = iota((pairs, 1), 0)
    lane_of_pair = iota((1, pairs), 1)
    shared_row = iota((8, 2 * lanes), 0)
    shared_lane = iota((8, 2 * lanes), 1)
    flat_rows = jnp.zeros((pairs, 1), jnp.int32)
    flat_lanes = jnp.zeros((1, pairs), jnp.int32)
    scalars = jnp.zeros((pairs, lanes), f32)
    shared = jnp.zeros((8, 2 * lanes), f32)
    first_scalar = 3 * heads * (steps - 1)
    for r in range(requests):
        tenant = tenant_ref[r]
        tokens = token_ref[tenant]
        slot = adapter_slot_ref[tenant_adapter_ref[tenant]]
        holder = slot // adapters_held
        position = seen[holder]
        seen[holder] = position + 1
        flat = (holder * capacity + position) * steps
        flat_rows = jnp.where(place // steps == r, flat, flat_rows)
        flat_lanes = jnp.where(lane_of_pair // steps == r, flat, flat_lanes)
        tenant_parts = [tenant // 16, tenant % 16]
        admits = [admitted_ref[s, r] for s in range(steps)]
        own = [slot - holder * adapters_held] + tenant_parts + [tokens // 32, tokens % 32] + admits
        line = jnp.zeros((1, lanes), jnp.int32)
        for index, value in enumerate(own):
            line = jnp.where(lane == first_scalar + index, value, line)
        scalars = jnp.where(place // steps == r, line.astype(f32), scalars)
        column = jnp.zeros((8, 2 * lanes), jnp.int32)
        for index, value in enumerate(tenant_parts + [length_ref[r]] + admits):
            column = jnp.where(shared_row == index, value, column)
        shared = jnp.where(shared_lane == me * requests + r, column.astype(f32), shared)
    flat_rows = flat_rows + place % steps
    flat_lanes = flat_lanes + lane_of_pair % steps
    back_ref[...] = one_hot(flat_rows, back_ref.shape)

    by_head = jnp.concatenate(
        [query_ref[:, h * width : (h + 1) * width] for h in range(heads)], axis=0
    )
    row = iota((total, total), 0)
    wanted = (row % heads) * pairs + ((row // heads) % steps) * requests + row // rows
    by_request = dot(one_hot(wanted, (total, total)), by_head).astype(bf16)
    new_scores = dot_t(by_request, new_key_ref[...]) * scale
    row = iota((total, 1), 0)
    new_column = iota((total, pairs), 1)
    by_step = [
        jnp.sum(
            jnp.where(new_column == j * requests + row // rows, new_scores, 0.0),
            axis=1,
            keepdims=True,
        )
        for j in range(steps)
    ]
    step_of_row = (row // heads) % steps
    own_score = by_step[0]
    for s in range(1, steps):
        own_score = jnp.where(step_of_row == s, by_step[s], own_score)
    own_place = new_column == step_of_row * requests + row // rows
    position = iota((rows, context), 1)
    copies[9].wait()
    copies[10].wait()
    for r in range(requests):
        block = pl.ds(r * rows, rows)
        scores = dot_t(by_request[r * rows : (r + 1) * rows], key_ref[r]) * scale
        scores = jnp.where(position < length_ref[r], scores, -jnp.inf)
        own = own_score[r * rows : (r + 1) * rows]
        top = jnp.maximum(jnp.max(scores, axis=1, keepdims=True), own)
        weight = jnp.exp(scores - top)
        own_weight = jnp.exp(own - top)
        mass = jnp.sum(weight, axis=1, keepdims=True) + own_weight
        inverse = 1.0 / mass
        attended[block, :] = dot((weight * inverse).astype(bf16), value_ref[r])
        own_exp[block, :] = jnp.broadcast_to(own_weight * inverse, (rows, lanes))
        masses[block, :] = jnp.broadcast_to(top + jnp.log(mass), (rows, lanes))
    own_weights = jnp.where(own_place, own_exp[:, 0:pairs], 0.0).astype(bf16)
    result = (attended[...] + dot(own_weights, new_value_ref[...])).astype(bf16)

    row = iota((total, total), 0)
    wanted = (row % pairs) * heads + row // pairs
    by_head = dot(one_hot(wanted, (total, total)), result).astype(bf16)
    for h in range(heads):
        home_ref[:, h * width : (h + 1) * width] = by_head[h * pairs : (h + 1) * pairs]
    place = iota((pairs, 1), 0)
    wanted = (place % steps) * requests + place // steps
    values = dot(one_hot(wanted, (pairs, pairs)), new_value_ref[...])
    home_ref[:, features : features + width] = values.astype(bf16)
    row = iota((total, 1), 0)
    lane = iota((total, lanes), 1)
    log_mass = masses[:, 0:1]
    pieces = jnp.zeros((total, lanes), f32)
    for j in range(steps - 1):
        rest = by_step[j] - log_mass
        for piece in range(3):
            part = rest.astype(bf16).astype(f32)
            rest = rest - part
            target = (piece * (steps - 1) + j) * heads + row % heads
            pieces = jnp.where(lane == target, part, pieces)
    gather = (iota((pairs, total), 1) // heads == iota((pairs, total), 0)).astype(f32).astype(bf16)
    scalars = scalars + dot(gather, pieces.astype(bf16))
    home_ref[:, features + width :] = scalars.astype(bf16)
    slots = send_ref.shape[0]
    pick = (iota((slots, pairs), 0) == flat_lanes).astype(f32).astype(bf16)
    sent = features + width + lanes
    send_ref[:, 0:sent] = dot(pick, home_ref[...]).astype(bf16)
    spread = (iota((slots, 8), 0) % 8 == iota((slots, 8), 1)).astype(f32).astype(bf16)
    send_ref[:, sent:] = dot(spread, shared.astype(bf16)).astype(bf16)
    copies[11].wait()


def combine_kernel(
    steps,
    heads,
    width,
    threshold,
    got_ref,
    home_ref,
    down_ref,
    weight_ref,
    low_ref,
    theirs_ref,
    final_ref,
    rows_ref,
):
    slots, pairs = got_ref.shape[0], home_ref.shape[0]
    features = heads * width
    sent = features + width + lanes
    count = slots + pairs
    shared = got_ref[0:8, sent:].astype(f32)
    for start in range(8, slots, 8):
        shared = shared + got_ref[start : start + 8, sent:].astype(f32)
    tenants = shared[0:1] * 16.0 + shared[1:2]
    charge_rows = []
    for s in range(steps - 1):
        charge = shared[2:3] + (s + 1.0)
        upper = jnp.floor(charge * (1.0 / 16.0))
        admitted = shared[3 + s : 4 + s]
        charge_rows += [upper * admitted, (charge - upper * 16.0) * admitted]
    charge_rows += [jnp.zeros_like(tenants)] * (8 - len(charge_rows))
    charges = jnp.concatenate(charge_rows, axis=0).astype(bf16)

    block = features + width
    scalars = jnp.concatenate(
        [got_ref[:, block:sent].astype(f32), home_ref[:, block:sent].astype(f32)], axis=0
    )
    first = 3 * heads * (steps - 1)
    tenant = scalars[:, first + 1 : first + 2] * 16.0 + scalars[:, first + 2 : first + 3]
    tokens = scalars[:, first + 3 : first + 4] * 32.0 + scalars[:, first + 4 : first + 5]
    same = (tenant == tenants).astype(f32).astype(bf16)
    grows = dot_t(same, charges)
    step_of_row = iota((count, 1), 0) % steps
    served_now = jnp.zeros((count, 1), f32)
    served = []
    for s in range(steps):
        open_now = (tokens < threshold).astype(f32)
        flag = open_now * scalars[:, first + 5 + s : first + 6 + s]
        served.append(flag)
        served_now = jnp.where(step_of_row == s, flag, served_now)
        if s + 1 < steps:
            grow = grows[:, 2 * s : 2 * s + 1] * 16.0 + grows[:, 2 * s + 1 : 2 * s + 2]
            tokens = tokens + open_now * grow

    span = heads * (steps - 1)
    logs = scalars[:, 0:span] + scalars[:, span : 2 * span] + scalars[:, 2 * span : 3 * span]
    shown = [(served[j] > 0.5) & (step_of_row > j) for j in range(steps - 1)]
    by_step = [
        jnp.where(shown[j], logs[:, j * heads : (j + 1) * heads], -jnp.inf)
        for j in range(steps - 1)
    ]
    top = jnp.zeros((count, heads), f32)
    for j in range(steps - 1):
        top = jnp.maximum(top, by_step[j])
    old = jnp.exp(-top)
    new = [jnp.exp(by_step[j] - top) for j in range(steps - 1)]
    mass = old
    for j in range(steps - 1):
        mass = mass + new[j]
    inverse = served_now / mass
    old = old * inverse
    new = [weight * inverse for weight in new]
    values = jnp.concatenate(
        [got_ref[:, features:block], home_ref[:, features:block]], axis=0
    )
    row = iota((count, 1), 0)
    new_values = [
        dot(one_hot(row - row % steps + j, (count, count)), values) for j in range(steps - 1)
    ]
    for h in range(heads):
        part = slice(h * width, (h + 1) * width)
        rows = jnp.concatenate([got_ref[:, part], home_ref[:, part]], axis=0).astype(f32)
        rows = rows * old[:, h : h + 1]
        for j in range(steps - 1):
            rows = rows + new_values[j] * new[j][:, h : h + 1]
        rows = rows.astype(bf16)
        rows_ref[:, part] = rows[0:slots]
        final_ref[:, part] = rows[slots:]

    rank = down_ref.shape[1]
    every = down_ref.shape[0] * rank
    product = dot_t(rows_ref[...], down_ref[...].reshape(every, features))
    owner = (iota(product.shape, 1) // rank).astype(f32)
    product = jnp.where(owner == scalars[0:slots, first : first + 1], product, 0.0)
    folded = product[:, 0:lanes]
    for start in range(lanes, every, lanes):
        folded = folded + product[:, start : start + lanes]
    folded = folded + pltpu.roll(folded, rank, 1)
    half = slots // 2
    low_half = iota((half, lanes), 1) < rank
    low_ref[...] = jnp.where(low_half, folded[0:half], folded[half:])
    project(1, final_ref, weight_ref, theirs_ref)


def project(flip, rows_ref, weight_ref, out_ref):
    parts, _, width = out_ref.shape
    core = lax.axis_index("core")
    mine = core if flip == 0 else 1 - core
    here = lax.axis_index("z")
    way = 1 - 2 * lax.rem(here, 2)
    for part in range(parts):
        target = lax.rem(here + way * part + parts, parts)
        start = pl.multiple_of((2 * target + mine) * width, width)
        product = dot(rows_ref[...], weight_ref[:, pl.ds(start, width)])
        out_ref[part] = product.astype(out_ref.dtype)


def mix_kernel(ours_ref, theirs_ref, low_ref, low_other_ref, low_out, base_out, first_out):
    low = (low_ref[...] + low_other_ref[...]).astype(bf16)
    for part in range(base_out.shape[0]):
        low_out[part] = low
        base_out[part] = (ours_ref[part] + theirs_ref[part].astype(f32)).astype(bf16)
    for index, part in enumerate((4, 3)):
        first_out[index] = base_out[part]


def hop_kernel(wanted, base_ref, came_ref, out_ref):
    for index, part in enumerate(wanted):
        total = came_ref[index].astype(f32) + base_ref[part].astype(f32)
        out_ref[index] = total.astype(bf16)


def late_hop_kernel(wanted, base_ref, came_ref, after_ref, out_ref):
    hop_kernel(wanted, base_ref, came_ref, out_ref)


def up_kernel(first_scalar, parts_ref, held_ref, up_ref, out_ref):
    rank = up_ref.shape[1]
    every = up_ref.shape[0] * rank
    low = parts_ref[0].astype(f32)
    for part in range(1, parts_ref.shape[0]):
        low = low + parts_ref[part].astype(f32)
    other = pltpu.roll(low, rank, 1)
    first = iota(low.shape, 1) < rank
    low = jnp.concatenate(
        [jnp.where(first, low, other), jnp.where(first, other, low)], axis=0
    )
    wide = jnp.concatenate([low] * (every // lanes), axis=1)
    owner = (iota(wide.shape, 1) // rank).astype(f32)
    held = held_ref[:, first_scalar : first_scalar + 1].astype(f32)
    wide = jnp.where(owner == held, wide, 0.0).astype(bf16)
    out_ref[...] = dot(wide, up_ref[...].reshape(every, up_ref.shape[2])).astype(bf16)


def finish_kernel(steps, base_ref, first_ref, second_ref, back_ref, term_ref, out_ref):
    pairs = out_ref.shape[0]
    total = base_ref[0].astype(f32) + first_ref[1].astype(f32) + second_ref[0].astype(f32)
    term = dot(back_ref[...], term_ref[...])
    rows = (total + adapter_scale * term).astype(bf16)
    place = iota((pairs, 1), 0)
    requests = pairs // steps
    wanted = (place % requests) * steps + place // requests
    out_ref[...] = dot(one_hot(wanted, (pairs, pairs)), rows).astype(bf16)


def per_device(
    queries,
    cache_keys,
    cache_values,
    new_keys,
    new_values,
    lengths,
    admitted,
    request_tenant,
    tenant_adapter,
    adapter_slot,
    tenant_tokens,
    out_weight,
    adapter_down_factor,
    adapter_up_factor,
):
    holders = lax.axis_size("batch")
    parts = lax.axis_size("z")
    steps, requests, features = queries.shape
    context, width = cache_keys.shape[1], cache_keys.shape[3]
    heads = features // width
    rows = steps * heads
    total = requests * rows
    pairs = steps * requests
    adapters_held, rank, _ = adapter_down_factor.shape
    every = adapters_held * rank
    threshold = float(3 * context)
    slots = holders * capacity * steps
    first_scalar = 3 * heads * (steps - 1)
    sent = features + width + lanes
    shape = jax.ShapeDtypeStruct

    home, send, back, weight = call(
        functools.partial(attend_kernel, steps, requests, heads, adapters_held),
        (
            shape((pairs, sent), bf16),
            shape((slots, sent + 2 * lanes), bf16),
            shape((pairs, slots), bf16),
            pltpu.VMEM(out_weight.shape, bf16),
        ),
        [HBM] * 12,
        (VMEM,) * 4,
        4 * total * context * width,
        4 * cache_keys.size,
        [
            pltpu.SMEM((requests,), jnp.int32),
            pltpu.SMEM((requests,), jnp.int32),
            pltpu.SMEM((steps, requests), jnp.int32),
            pltpu.SMEM(tenant_adapter.shape, jnp.int32),
            pltpu.SMEM(adapter_slot.shape, jnp.int32),
            pltpu.SMEM(tenant_tokens.shape, jnp.int32),
            pltpu.SMEM((holders,), jnp.int32),
            pltpu.VMEM((pairs, features), bf16),
            pltpu.VMEM((requests, context, width), bf16),
            pltpu.VMEM((requests, context, width), bf16),
            pltpu.VMEM((pairs, width), bf16),
            pltpu.VMEM((pairs, width), bf16),
            pltpu.VMEM((total, width), f32),
            pltpu.VMEM((total, lanes), f32),
            pltpu.VMEM((total, lanes), f32),
            pltpu.SemaphoreType.DMA((12,)),
        ],
        40 << 20,
    )(
        *map(
            in_hbm,
            (
                request_tenant,
                lengths,
                admitted,
                tenant_adapter,
                adapter_slot,
                tenant_tokens,
                queries.reshape(pairs, features),
                cache_keys.reshape(requests, context, width),
                cache_values.reshape(requests, context, width),
                new_keys.reshape(pairs, width),
                new_values.reshape(pairs, width),
                out_weight,
            ),
        )
    )
    got = lax.all_to_all(send, "batch", split_axis=0, concat_axis=0, tiled=True)
    low, theirs, final = call(
        functools.partial(combine_kernel, steps, heads, width, threshold),
        (
            shape((slots // 2, lanes), f32),
            shape((parts, pairs, features), bf16),
            shape((pairs, features), bf16),
        ),
        [VMEM] * 4,
        (VMEM,) * 3,
        2 * slots * features * every,
        out_weight.size,
        [pltpu.VMEM((slots, features), bf16)],
    )(got, home, adapter_down_factor, in_vmem(weight))
    swap = [(0, 1), (1, 0)]
    low_other = lax.ppermute(low, "core", swap)
    theirs = lax.ppermute(theirs, "core", swap)
    ours = call(
        functools.partial(project, 0),
        shape((parts, pairs, features), f32),
        [VMEM] * 2,
        VMEM,
        pairs * out_weight.size,
        out_weight.size,
    )(final, in_vmem(weight))
    two = shape((2, pairs, features), bf16)
    one = shape((1, pairs, features), bf16)
    low, base, sums = call(
        mix_kernel,
        (
            shape((parts, slots // 2, lanes), bf16),
            shape((parts, pairs, features), bf16),
            two,
        ),
        [VMEM] * 4,
        (VMEM,) * 3,
        2 * ours.size,
        8 * ours.size,
    )(ours, theirs, low, low_other)
    low = lax.all_to_all(low, "z", split_axis=0, concat_axis=0, tiled=True)

    def hop(kernel, wanted, out, *args):
        return call(
            functools.partial(kernel, wanted),
            out,
            [VMEM, VMEM] + [HBM] * (len(args) - 2),
            VMEM,
            out.size,
            6 * out.size,
        )(*args)

    odd = [(i, i + 1 - 2 * (i % 2)) for i in range(parts)]
    even = [(i, (i - 1 + 2 * (i % 2)) % parts) for i in range(parts)]
    sums = lax.ppermute(sums, "z", odd)
    sums = lax.ppermute(hop(hop_kernel, (5, 6), two, base, sums), "z", even)
    term = call(
        functools.partial(up_kernel, first_scalar),
        shape((slots, features), bf16),
        [VMEM] * 3,
        VMEM,
        2 * slots * features * every,
        4 * slots * features,
    )(low, got[:, features + width : sent], adapter_up_factor)
    sums = hop(late_hop_kernel, (2, 1), two, base, sums, term)
    sums = lax.ppermute(sums, "z", odd)
    last = lax.ppermute(hop(hop_kernel, (7,), one, base, sums), "z", even)
    term = lax.all_to_all(term, "batch", split_axis=0, concat_axis=0, tiled=True)
    out = call(
        functools.partial(finish_kernel, steps),
        shape((pairs, features), bf16),
        [VMEM] * 5,
        VMEM,
        2 * pairs * slots * features,
        10 * one.size,
    )(base, sums, last, back, term)
    return out.reshape(steps, requests, features)


def solution(mesh):
    batch, tensor = mesh.shape["batch"], mesh.shape["tensor"]
    split = Mesh(mesh.devices.reshape(batch, tensor // 2, 2), ("batch", "z", "core"))
    tensor_axes = ("z", "core")
    placed = (
        P(None, "batch", tensor_axes),
        P("batch", None, tensor_axes, None),
        P("batch", None, tensor_axes, None),
        P(None, "batch", tensor_axes, None),
        P(None, "batch", tensor_axes, None),
        P("batch"),
        P(None, "batch"),
        P("batch"),
        P(),
        P(),
        P(),
        P(tensor_axes, None),
        P("batch", None, tensor_axes),
        P("batch", None, tensor_axes),
    )
    return jax.shard_map(
        per_device,
        mesh=split,
        in_specs=placed,
        out_specs=P(None, "batch", tensor_axes),
        check_vma=False,
    )
```

```python
import functools

import jax
import jax.numpy as jnp
from jax import lax
from jax.experimental import pallas as pl
from jax.experimental.pallas import tpu as pltpu
from jax.sharding import Mesh
from jax.sharding import PartitionSpec as P

adapter_scale = 2.0
capacity = 2
lanes = 128
first_blocks = (4, 3)
other_blocks = (5, 6, 2, 1, 7, 0)
f32 = jnp.float32
bf16 = jnp.bfloat16
VMEM = pl.BlockSpec(memory_space=pltpu.VMEM)
SMEM = pl.BlockSpec(memory_space=pltpu.SMEM)
HBM = pl.BlockSpec(memory_space=pltpu.HBM)


def in_hbm(array):
    return pltpu.with_memory_space_constraint(array, pltpu.HBM)


def in_vmem(array):
    return pltpu.with_memory_space_constraint(array, pltpu.VMEM)


def iota(shape, axis):
    return lax.broadcasted_iota(jnp.int32, shape, axis)


def dot(a, b):
    return jnp.dot(a, b, preferred_element_type=f32)


def dot_t(a, b):
    return lax.dot_general(a, b, (((1,), (1,)), ((), ())), preferred_element_type=f32)


def call(kernel, out_shape, in_specs, out_specs, flops, moved, scratch=(), limit=16 << 20):
    return pl.pallas_call(
        kernel,
        out_shape=out_shape,
        in_specs=in_specs,
        out_specs=out_specs,
        scratch_shapes=list(scratch),
        cost_estimate=pl.CostEstimate(flops=flops, bytes_accessed=moved, transcendentals=0),
        compiler_params=pltpu.CompilerParams(vmem_limit_bytes=limit),
    )


def fetch_all(pairs, sems):
    copies = []
    for index, (source, target) in enumerate(pairs):
        copy = pltpu.make_async_copy(source, target, sems.at[index])
        copy.start()
        copies.append(copy)
    return copies


def one_hot(wanted, shape):
    return (wanted == iota(shape, 1)).astype(f32).astype(bf16)


def attend_kernel(
    steps,
    requests,
    heads,
    adapters_held,
    tenant_in,
    length_in,
    admitted_in,
    tenant_adapter_in,
    adapter_slot_in,
    token_in,
    query_in,
    key_in,
    value_in,
    new_key_in,
    new_value_in,
    projection_in,
    home_ref,
    send_ref,
    back_ref,
    projection_ref,
    tenant_ref,
    length_ref,
    admitted_ref,
    tenant_adapter_ref,
    adapter_slot_ref,
    token_ref,
    seen,
    query_ref,
    key_ref,
    value_ref,
    new_key_ref,
    new_value_ref,
    attended,
    score_ref,
    weight_ref,
    sems,
):
    rows = steps * heads
    total = requests * rows
    pairs = steps * requests
    width = key_ref.shape[2]
    context = key_ref.shape[1]
    features = heads * width
    scale = width ** (-0.5)
    copies = fetch_all(
        [
            (tenant_in, tenant_ref),
            (length_in, length_ref),
            (admitted_in, admitted_ref),
            (tenant_adapter_in, tenant_adapter_ref),
            (adapter_slot_in, adapter_slot_ref),
            (token_in, token_ref),
            (query_in, query_ref),
            (new_key_in, new_key_ref),
            (new_value_in, new_value_ref),
            (key_in, key_ref),
            (value_in, value_ref),
            (projection_in, projection_ref),
        ],
        sems,
    )
    for index in range(seen.shape[0]):
        seen[index] = 0
    for copy in copies[:9]:
        copy.wait()

    lane = iota((1, lanes), 1)
    place = iota((pairs, 1), 0)
    lane_of_pair = iota((1, pairs), 1)
    shared_row = iota((8, lanes), 0)
    shared_lane = iota((8, lanes), 1)
    flat_rows = jnp.zeros((pairs, 1), jnp.int32)
    flat_lanes = jnp.zeros((1, pairs), jnp.int32)
    scalars = jnp.zeros((pairs, lanes), f32)
    shared = jnp.zeros((8, lanes), f32)
    first_scalar = 3 * heads * (steps - 1)
    for r in range(requests):
        tenant = tenant_ref[r]
        tokens = token_ref[tenant]
        slot = adapter_slot_ref[tenant_adapter_ref[tenant]]
        holder = slot // adapters_held
        position = seen[holder]
        seen[holder] = position + 1
        flat = (holder * capacity + position) * steps
        flat_rows = jnp.where(place % requests == r, flat, flat_rows)
        flat_lanes = jnp.where(lane_of_pair % requests == r, flat, flat_lanes)
        tenant_parts = [tenant // 16, tenant % 16]
        admits = [admitted_ref[s, r] for s in range(steps)]
        own = [slot - holder * adapters_held] + tenant_parts + [tokens // 32, tokens % 32] + admits
        line = jnp.zeros((1, lanes), jnp.int32)
        for index, value in enumerate(own):
            line = jnp.where(lane == first_scalar + index, value, line)
        scalars = jnp.where(place % requests == r, line.astype(f32), scalars)
        column = jnp.zeros((8, lanes), jnp.int32)
        for index, value in enumerate(tenant_parts + [length_ref[r]] + admits):
            column = jnp.where(shared_row == index, value, column)
        shared = jnp.where(shared_lane == lanes // 2 + r, column.astype(f32), shared)
    flat_rows = flat_rows + place // requests
    flat_lanes = flat_lanes + lane_of_pair // requests
    back_ref[...] = one_hot(flat_rows, back_ref.shape)

    by_head = jnp.concatenate(
        [query_ref[:, h * width : (h + 1) * width] for h in range(heads)], axis=0
    )
    row = iota((total, total), 0)
    wanted = (row % heads) * pairs + ((row // heads) % steps) * requests + row // rows
    by_request = dot(one_hot(wanted, (total, total)), by_head).astype(bf16)
    new_scores = dot_t(by_request, new_key_ref[...]) * scale
    row = iota((total, 1), 0)
    new_column = iota((total, pairs), 1)
    by_step = [
        jnp.sum(
            jnp.where(new_column == j * requests + row // rows, new_scores, 0.0),
            axis=1,
            keepdims=True,
        )
        for j in range(steps)
    ]
    step_of_row = (row // heads) % steps
    own_score = by_step[0]
    for s in range(1, steps):
        own_score = jnp.where(step_of_row == s, by_step[s], own_score)
    own_place = new_column == step_of_row * requests + row // rows
    position = iota((rows, context), 1)
    copies[9].wait()
    for r in range(requests):
        block = slice(r * rows, (r + 1) * rows)
        scores = dot_t(by_request[block], key_ref[r]) * scale
        score_ref[block, :] = jnp.where(position < length_ref[r], scores, -jnp.inf)
    scores = score_ref[...]
    top = jnp.maximum(jnp.max(scores, axis=1, keepdims=True), own_score)
    weight = jnp.exp(scores - top)
    own_weight = jnp.exp(own_score - top)
    mass = jnp.sum(weight, axis=1, keepdims=True) + own_weight
    inverse = 1.0 / mass
    log_mass = top + jnp.log(mass)
    weight_ref[...] = (weight * inverse).astype(bf16)
    copies[10].wait()
    for r in range(requests):
        block = slice(r * rows, (r + 1) * rows)
        attended[block, :] = dot(weight_ref[block, :], value_ref[r])
    own_weights = jnp.where(own_place, own_weight * inverse, 0.0).astype(bf16)
    result = (attended[...] + dot(own_weights, new_value_ref[...])).astype(bf16)

    row = iota((total, total), 0)
    wanted = (row % requests) * rows + ((row // requests) % steps) * heads + row // pairs
    by_head = dot(one_hot(wanted, (total, total)), result).astype(bf16)
    for h in range(heads):
        home_ref[:, h * width : (h + 1) * width] = by_head[h * pairs : (h + 1) * pairs]
    home_ref[:, features : features + width] = new_value_ref[...]
    row = iota((total, 1), 0)
    lane = iota((total, lanes), 1)
    pieces = jnp.zeros((total, lanes), f32)
    for j in range(steps - 1):
        rest = by_step[j] - log_mass
        for piece in range(3):
            part = rest.astype(bf16).astype(f32)
            rest = rest - part
            target = (piece * (steps - 1) + j) * heads + row % heads
            pieces = jnp.where(lane == target, part, pieces)
    column = iota((pairs, total), 1)
    wanted = ((column // heads) % steps) * requests + column // rows
    gather = (wanted == iota((pairs, total), 0)).astype(f32).astype(bf16)
    scalars = scalars + dot(gather, pieces.astype(bf16))
    home_ref[:, features + width :] = scalars.astype(bf16)
    slots = send_ref.shape[0]
    pick = (iota((slots, pairs), 0) == flat_lanes).astype(f32).astype(bf16)
    block = features + width
    picked = dot(pick, home_ref[...])
    spread = (iota((slots, 8), 0) % 8 == iota((slots, 8), 1)).astype(f32).astype(bf16)
    send_ref[:, 0:block] = picked[:, 0:block].astype(bf16)
    integers = dot(spread, shared.astype(bf16))
    send_ref[:, block:] = (picked[:, block:] + integers).astype(bf16)
    copies[11].wait()


def combine_kernel(
    steps,
    heads,
    width,
    threshold,
    got_ref,
    home_ref,
    down_ref,
    weight_ref,
    low_ref,
    theirs_ref,
    others_ref,
    final_ref,
    rows_ref,
):
    slots, pairs = got_ref.shape[0], home_ref.shape[0]
    features = heads * width
    sent = features + width + lanes
    count = slots + pairs
    block = features + width
    requests = pairs // steps
    everyone = requests * (slots // 8)
    column = iota((lanes, everyone), 1)
    tile = (iota((lanes, everyone), 0) == lanes // 2 + column % requests).astype(f32).astype(bf16)
    column = iota((slots, everyone), 1)
    from_row = column // requests == iota((slots, everyone), 0) // 8
    tiled = jnp.where(from_row, dot(got_ref[:, block:], tile), 0.0).astype(bf16)
    kind = (iota((8, slots), 1) % 8 == iota((8, slots), 0)).astype(f32).astype(bf16)
    shared = dot(kind, tiled)
    tenants = shared[0:1] * 16.0 + shared[1:2]
    charge_rows = []
    for s in range(steps - 1):
        charge = shared[2:3] + (s + 1.0)
        upper = jnp.floor(charge * (1.0 / 16.0))
        admitted = shared[3 + s : 4 + s]
        charge_rows += [upper * admitted, (charge - upper * 16.0) * admitted]
    charge_rows += [jnp.zeros_like(tenants)] * (8 - len(charge_rows))
    charges = jnp.concatenate(charge_rows, axis=0).astype(bf16)

    scalars = jnp.concatenate(
        [got_ref[:, block:sent].astype(f32), home_ref[:, block:sent].astype(f32)], axis=0
    )
    first = 3 * heads * (steps - 1)
    tenant = scalars[:, first + 1 : first + 2] * 16.0 + scalars[:, first + 2 : first + 3]
    tokens = scalars[:, first + 3 : first + 4] * 32.0 + scalars[:, first + 4 : first + 5]
    same = (tenant == tenants).astype(f32).astype(bf16)
    grows = dot_t(same, charges)
    row = iota((count, 1), 0)
    step_of_row = jnp.where(row < slots, row % steps, (row - slots) // requests)
    served_now = jnp.zeros((count, 1), f32)
    served = []
    for s in range(steps):
        open_now = (tokens < threshold).astype(f32)
        flag = open_now * scalars[:, first + 5 + s : first + 6 + s]
        served.append(flag)
        served_now = jnp.where(step_of_row == s, flag, served_now)
        if s + 1 < steps:
            grow = grows[:, 2 * s : 2 * s + 1] * 16.0 + grows[:, 2 * s + 1 : 2 * s + 2]
            tokens = tokens + open_now * grow

    span = heads * (steps - 1)
    logs = scalars[:, 0:span] + scalars[:, span : 2 * span] + scalars[:, 2 * span : 3 * span]
    shown = [(served[j] > 0.5) & (step_of_row > j) for j in range(steps - 1)]
    by_step = [
        jnp.where(shown[j], logs[:, j * heads : (j + 1) * heads], -jnp.inf)
        for j in range(steps - 1)
    ]
    top = jnp.zeros((count, heads), f32)
    for j in range(steps - 1):
        top = jnp.maximum(top, by_step[j])
    old = jnp.exp(-top)
    new = [jnp.exp(by_step[j] - top) for j in range(steps - 1)]
    mass = old
    for j in range(steps - 1):
        mass = mass + new[j]
    inverse = served_now / mass
    old = old * inverse
    new = [weight * inverse for weight in new]
    values = jnp.concatenate(
        [got_ref[:, features:block], home_ref[:, features:block]], axis=0
    )
    first_row = jnp.where(row < slots, row - row % steps, slots + (row - slots) % requests)
    stride = jnp.where(row < slots, 1, requests)
    new_values = [
        dot(one_hot(first_row + stride * j, (count, count)), values) for j in range(steps - 1)
    ]
    for h in range(heads):
        part = slice(h * width, (h + 1) * width)
        rows = jnp.concatenate([got_ref[:, part], home_ref[:, part]], axis=0).astype(f32)
        rows = rows * old[:, h : h + 1]
        for j in range(steps - 1):
            rows = rows + new_values[j] * new[j][:, h : h + 1]
        rows = rows.astype(bf16)
        rows_ref[:, part] = rows[0:slots]
        final_ref[:, part] = rows[slots:]

    rank = down_ref.shape[1]
    every = down_ref.shape[0] * rank
    product = dot_t(rows_ref[...], down_ref[...].reshape(every, features))
    owner = (iota(product.shape, 1) // rank).astype(f32)
    product = jnp.where(owner == scalars[0:slots, first : first + 1], product, 0.0)
    folded = product[:, 0:lanes]
    for start in range(lanes, every, lanes):
        folded = folded + product[:, start : start + lanes]
    folded = folded + pltpu.roll(folded, rank, 1)
    half = slots // 2
    low_half = iota((half, lanes), 1) < rank
    low = jnp.where(low_half, folded[0:half], folded[half:])
    low_ref[...] = low
    for index, product in enumerate(project(1, first_blocks, final_ref, weight_ref)):
        theirs_ref[:, index * features : (index + 1) * features] = product.astype(bf16)
    start = len(first_blocks) * features
    upper = low.astype(bf16)
    theirs_ref[:, start : start + lanes] = upper
    theirs_ref[:, start + lanes :] = (low - upper.astype(f32)).astype(bf16)
    for index, product in enumerate(project(1, other_blocks, final_ref, weight_ref)):
        others_ref[index] = product.astype(bf16)


def project(flip, wanted, rows_ref, weight_ref):
    parts = lax.axis_size("z")
    width = weight_ref.shape[1] // (2 * parts)
    core = lax.axis_index("core")
    mine = core if flip == 0 else 1 - core
    here = lax.axis_index("z")
    way = 1 - 2 * lax.rem(here, 2)
    products = []
    for part in wanted:
        target = lax.rem(here + way * part + parts, parts)
        start = pl.multiple_of((2 * target + mine) * width, width)
        products.append(dot(rows_ref[...], weight_ref[:, pl.ds(start, width)]))
    return products


def ours_kernel(rows_ref, weight_ref, out_ref):
    blocks = first_blocks + other_blocks
    for index, product in enumerate(project(0, blocks, rows_ref, weight_ref)):
        out_ref[index] = product


def mix_kernel(low_ref, ours_ref, came_ref, low_out, first_out):
    count, _, width = first_out.shape
    start = count * width
    other = came_ref[:, start : start + lanes].astype(f32)
    other = other + came_ref[:, start + lanes :].astype(f32)
    low = (low_ref[...] + other).astype(bf16)
    for part in range(low_out.shape[0]):
        low_out[part] = low
    for index in range(count):
        came = came_ref[:, index * width : (index + 1) * width].astype(f32)
        first_out[index] = (ours_ref[index] + came).astype(bf16)


def hop_kernel(first, ours_ref, others_ref, came_ref, out_ref):
    skip = len(first_blocks) + first
    for index in range(out_ref.shape[0]):
        here = ours_ref[skip + index] + others_ref[first + index].astype(f32)
        out_ref[index] = (came_ref[index].astype(f32) + here).astype(bf16)


def late_hop_kernel(first, ours_ref, others_ref, came_ref, after_ref, out_ref):
    hop_kernel(first, ours_ref, others_ref, came_ref, out_ref)


def up_kernel(first_scalar, parts_ref, held_ref, up_ref, out_ref):
    rank = up_ref.shape[1]
    every = up_ref.shape[0] * rank
    low = parts_ref[0].astype(f32)
    for part in range(1, parts_ref.shape[0]):
        low = low + parts_ref[part].astype(f32)
    other = pltpu.roll(low, rank, 1)
    first = iota(low.shape, 1) < rank
    low = jnp.concatenate(
        [jnp.where(first, low, other), jnp.where(first, other, low)], axis=0
    )
    wide = jnp.concatenate([low] * (every // lanes), axis=1)
    owner = (iota(wide.shape, 1) // rank).astype(f32)
    held = held_ref[:, first_scalar : first_scalar + 1].astype(f32)
    wide = jnp.where(owner == held, wide, 0.0).astype(bf16)
    out_ref[...] = dot(wide, up_ref[...].reshape(every, up_ref.shape[2])).astype(bf16)


def finish_kernel(ours_ref, others_ref, first_ref, second_ref, back_ref, term_ref, out_ref):
    total = ours_ref[0] + others_ref[0].astype(f32)
    total = total + first_ref[0].astype(f32) + second_ref[0].astype(f32)
    term = dot(back_ref[...], term_ref[...])
    out_ref[...] = (total + adapter_scale * term).astype(bf16)


def per_device(
    queries,
    cache_keys,
    cache_values,
    new_keys,
    new_values,
    lengths,
    admitted,
    request_tenant,
    tenant_adapter,
    adapter_slot,
    tenant_tokens,
    out_weight,
    adapter_down_factor,
    adapter_up_factor,
):
    holders = lax.axis_size("batch")
    parts = lax.axis_size("z")
    steps, requests, features = queries.shape
    context, width = cache_keys.shape[1], cache_keys.shape[3]
    heads = features // width
    rows = steps * heads
    total = requests * rows
    pairs = steps * requests
    adapters_held, rank, _ = adapter_down_factor.shape
    every = adapters_held * rank
    threshold = float(3 * context)
    slots = holders * capacity * steps
    first_scalar = 3 * heads * (steps - 1)
    sent = features + width + lanes
    shape = jax.ShapeDtypeStruct

    home, send, back, weight = call(
        functools.partial(attend_kernel, steps, requests, heads, adapters_held),
        (
            shape((pairs, sent), bf16),
            shape((slots, sent), bf16),
            shape((pairs, slots), bf16),
            pltpu.VMEM(out_weight.shape, bf16),
        ),
        [HBM] * 12,
        (VMEM,) * 4,
        4 * total * context * width,
        4 * cache_keys.size,
        [
            pltpu.SMEM((requests,), jnp.int32),
            pltpu.SMEM((requests,), jnp.int32),
            pltpu.SMEM((steps, requests), jnp.int32),
            pltpu.SMEM(tenant_adapter.shape, jnp.int32),
            pltpu.SMEM(adapter_slot.shape, jnp.int32),
            pltpu.SMEM(tenant_tokens.shape, jnp.int32),
            pltpu.SMEM((holders,), jnp.int32),
            pltpu.VMEM((pairs, features), bf16),
            pltpu.VMEM((requests, context, width), bf16),
            pltpu.VMEM((requests, context, width), bf16),
            pltpu.VMEM((pairs, width), bf16),
            pltpu.VMEM((pairs, width), bf16),
            pltpu.VMEM((total, width), f32),
            pltpu.VMEM((total, context), f32),
            pltpu.VMEM((total, context), bf16),
            pltpu.SemaphoreType.DMA((12,)),
        ],
        40 << 20,
    )(
        *map(
            in_hbm,
            (
                request_tenant,
                lengths,
                admitted,
                tenant_adapter,
                adapter_slot,
                tenant_tokens,
                queries.reshape(pairs, features),
                cache_keys.reshape(requests, context, width),
                cache_values.reshape(requests, context, width),
                new_keys.reshape(pairs, width),
                new_values.reshape(pairs, width),
                out_weight,
            ),
        )
    )
    got = lax.all_to_all(send, "batch", split_axis=0, concat_axis=0, tiled=True)
    weight = in_vmem(weight)
    two = shape((2, pairs, features), bf16)
    one = shape((1, pairs, features), bf16)
    six = shape((len(other_blocks), pairs, features), bf16)
    blocks = shape((parts, pairs, features), f32)
    low, theirs, others, final = call(
        functools.partial(combine_kernel, steps, heads, width, threshold),
        (
            shape((slots // 2, lanes), f32),
            shape((pairs, 2 * features + 2 * lanes), bf16),
            six,
            shape((pairs, features), bf16),
        ),
        [VMEM] * 4,
        (VMEM,) * 4,
        2 * slots * features * every,
        out_weight.size,
        [pltpu.VMEM((slots, features), bf16)],
    )(got, home, adapter_down_factor, weight)
    swap = [(0, 1), (1, 0)]
    theirs = lax.ppermute(theirs, "core", swap)
    others = lax.ppermute(others, "core", swap)
    ours = call(
        ours_kernel,
        blocks,
        [VMEM] * 2,
        VMEM,
        pairs * out_weight.size,
        out_weight.size,
    )(final, weight)
    low, sums = call(
        mix_kernel,
        (shape((parts, slots // 2, lanes), bf16), two),
        [VMEM] * 3,
        (VMEM,) * 2,
        2 * two.size,
        8 * two.size,
    )(low, ours, theirs)
    low = lax.all_to_all(low, "z", split_axis=0, concat_axis=0, tiled=True)

    def hop(kernel, first, out, *args):
        return call(
            functools.partial(kernel, first),
            out,
            [VMEM] * 3 + [HBM] * (len(args) - 3),
            VMEM,
            out.size,
            6 * out.size,
        )(*args)

    odd = [(i, i + 1 - 2 * (i % 2)) for i in range(parts)]
    even = [(i, (i - 1 + 2 * (i % 2)) % parts) for i in range(parts)]
    sums = lax.ppermute(sums, "z", odd)
    sums = lax.ppermute(hop(hop_kernel, 0, two, ours, others, sums), "z", even)
    term = call(
        functools.partial(up_kernel, first_scalar),
        shape((slots, features), bf16),
        [VMEM] * 3,
        VMEM,
        2 * slots * features * every,
        4 * slots * features,
    )(low, got[:, features + width : sent], adapter_up_factor)
    sums = hop(late_hop_kernel, 2, two, ours, others, sums, term)
    sums = lax.ppermute(sums, "z", odd)
    last = lax.ppermute(hop(hop_kernel, 4, one, ours, others, sums), "z", even)
    term = lax.all_to_all(term, "batch", split_axis=0, concat_axis=0, tiled=True)
    out = call(
        finish_kernel,
        shape((pairs, features), bf16),
        [VMEM] * 6,
        VMEM,
        2 * pairs * slots * features,
        10 * one.size,
    )(ours[-1:], others[-1:], sums[1:], last, back, term)
    return out.reshape(steps, requests, features)


def solution(mesh):
    batch, tensor = mesh.shape["batch"], mesh.shape["tensor"]
    split = Mesh(mesh.devices.reshape(batch, tensor // 2, 2), ("batch", "z", "core"))
    tensor_axes = ("z", "core")
    placed = (
        P(None, "batch", tensor_axes),
        P("batch", None, tensor_axes, None),
        P("batch", None, tensor_axes, None),
        P(None, "batch", tensor_axes, None),
        P(None, "batch", tensor_axes, None),
        P("batch"),
        P(None, "batch"),
        P("batch"),
        P(),
        P(),
        P(),
        P(tensor_axes, None),
        P("batch", None, tensor_axes),
        P("batch", None, tensor_axes),
    )
    return jax.shard_map(
        per_device,
        mesh=split,
        in_specs=placed,
        out_specs=P(None, "batch", tensor_axes),
        check_vma=False,
    )
```

```python
import functools

import jax
import jax.numpy as jnp
from jax import lax
from jax.experimental import pallas as pl
from jax.experimental.pallas import tpu as pltpu
from jax.sharding import Mesh
from jax.sharding import PartitionSpec as P

adapter_scale = 2.0
capacity = 2
lanes = 128
first_blocks = (4, 3)
other_blocks = (5, 6, 2, 1, 7, 0)
f32 = jnp.float32
bf16 = jnp.bfloat16
VMEM = pl.BlockSpec(memory_space=pltpu.VMEM)
SMEM = pl.BlockSpec(memory_space=pltpu.SMEM)
HBM = pl.BlockSpec(memory_space=pltpu.HBM)


def in_hbm(array):
    return pltpu.with_memory_space_constraint(array, pltpu.HBM)


def in_vmem(array):
    return pltpu.with_memory_space_constraint(array, pltpu.VMEM)


def iota(shape, axis):
    return lax.broadcasted_iota(jnp.int32, shape, axis)


def dot(a, b):
    return jnp.dot(a, b, preferred_element_type=f32)


def dot_t(a, b):
    return lax.dot_general(a, b, (((1,), (1,)), ((), ())), preferred_element_type=f32)


def call(kernel, out_shape, in_specs, out_specs, flops, moved, scratch=(), limit=16 << 20):
    return pl.pallas_call(
        kernel,
        out_shape=out_shape,
        in_specs=in_specs,
        out_specs=out_specs,
        scratch_shapes=list(scratch),
        cost_estimate=pl.CostEstimate(flops=flops, bytes_accessed=moved, transcendentals=0),
        compiler_params=pltpu.CompilerParams(vmem_limit_bytes=limit),
    )


def fetch_all(pairs, sems):
    copies = []
    for index, (source, target) in enumerate(pairs):
        copy = pltpu.make_async_copy(source, target, sems.at[index])
        copy.start()
        copies.append(copy)
    return copies


def one_hot(wanted, shape):
    return (wanted == iota(shape, 1)).astype(f32).astype(bf16)


def attend_kernel(
    steps,
    requests,
    heads,
    adapters_held,
    tenant_in,
    length_in,
    admitted_in,
    tenant_adapter_in,
    adapter_slot_in,
    token_in,
    query_in,
    key_in,
    value_in,
    new_key_in,
    new_value_in,
    projection_in,
    home_ref,
    send_ref,
    back_ref,
    projection_ref,
    tenant_ref,
    length_ref,
    admitted_ref,
    tenant_adapter_ref,
    adapter_slot_ref,
    token_ref,
    seen,
    query_ref,
    key_ref,
    value_ref,
    new_key_ref,
    new_value_ref,
    attended,
    score_ref,
    weight_ref,
    sems,
):
    rows = steps * heads
    total = requests * rows
    pairs = steps * requests
    width = key_ref.shape[2]
    context = key_ref.shape[1]
    features = heads * width
    scale = width ** (-0.5)
    copies = fetch_all(
        [
            (tenant_in, tenant_ref),
            (length_in, length_ref),
            (admitted_in, admitted_ref),
            (tenant_adapter_in, tenant_adapter_ref),
            (adapter_slot_in, adapter_slot_ref),
            (token_in, token_ref),
            (query_in, query_ref),
            (new_key_in, new_key_ref),
            (new_value_in, new_value_ref),
            (key_in, key_ref),
            (value_in, value_ref),
            (projection_in.at[pl.ds(0, projection_ref.shape[0])], projection_ref),
        ],
        sems,
    )
    for index in range(seen.shape[0]):
        seen[index] = 0
    for copy in copies[:9]:
        copy.wait()

    lane = iota((1, lanes), 1)
    place = iota((pairs, 1), 0)
    lane_of_pair = iota((1, pairs), 1)
    shared_row = iota((8, lanes), 0)
    shared_lane = iota((8, lanes), 1)
    flat_rows = jnp.zeros((pairs, 1), jnp.int32)
    flat_lanes = jnp.zeros((1, pairs), jnp.int32)
    scalars = jnp.zeros((pairs, lanes), f32)
    shared = jnp.zeros((8, lanes), f32)
    first_scalar = 3 * heads * (steps - 1)
    for r in range(requests):
        tenant = tenant_ref[r]
        tokens = token_ref[tenant]
        slot = adapter_slot_ref[tenant_adapter_ref[tenant]]
        holder = slot // adapters_held
        position = seen[holder]
        seen[holder] = position + 1
        flat = (holder * capacity + position) * steps
        flat_rows = jnp.where(place % requests == r, flat, flat_rows)
        flat_lanes = jnp.where(lane_of_pair % requests == r, flat, flat_lanes)
        tenant_parts = [tenant // 16, tenant % 16]
        admits = [admitted_ref[s, r] for s in range(steps)]
        own = [slot - holder * adapters_held] + tenant_parts + [tokens // 32, tokens % 32] + admits
        line = jnp.zeros((1, lanes), jnp.int32)
        for index, value in enumerate(own):
            line = jnp.where(lane == first_scalar + index, value, line)
        scalars = jnp.where(place % requests == r, line.astype(f32), scalars)
        column = jnp.zeros((8, lanes), jnp.int32)
        for index, value in enumerate(tenant_parts + [length_ref[r]] + admits):
            column = jnp.where(shared_row == index, value, column)
        shared = jnp.where(shared_lane == lanes // 2 + r, column.astype(f32), shared)
    flat_rows = flat_rows + place // requests
    flat_lanes = flat_lanes + lane_of_pair // requests
    back_ref[...] = one_hot(flat_rows, back_ref.shape)

    by_head = jnp.concatenate(
        [query_ref[:, h * width : (h + 1) * width] for h in range(heads)], axis=0
    )
    row = iota((total, total), 0)
    wanted = (row % heads) * pairs + ((row // heads) % steps) * requests + row // rows
    by_request = dot(one_hot(wanted, (total, total)), by_head).astype(bf16)
    new_scores = dot_t(by_request, new_key_ref[...]) * scale
    row = iota((total, 1), 0)
    new_column = iota((total, pairs), 1)
    by_step = [
        jnp.sum(
            jnp.where(new_column == j * requests + row // rows, new_scores, 0.0),
            axis=1,
            keepdims=True,
        )
        for j in range(steps)
    ]
    step_of_row = (row // heads) % steps
    own_score = by_step[0]
    for s in range(1, steps):
        own_score = jnp.where(step_of_row == s, by_step[s], own_score)
    own_place = new_column == step_of_row * requests + row // rows
    position = iota((rows, context), 1)
    copies[9].wait()
    for r in range(requests):
        block = slice(r * rows, (r + 1) * rows)
        scores = dot_t(by_request[block], key_ref[r]) * scale
        score_ref[block, :] = jnp.where(position < length_ref[r], scores, -jnp.inf)
    scores = score_ref[...]
    top = jnp.maximum(jnp.max(scores, axis=1, keepdims=True), own_score)
    weight = jnp.exp(scores - top)
    own_weight = jnp.exp(own_score - top)
    mass = jnp.sum(weight, axis=1, keepdims=True) + own_weight
    inverse = 1.0 / mass
    log_mass = top + jnp.log(mass)
    weight_ref[...] = (weight * inverse).astype(bf16)
    copies[10].wait()
    for r in range(requests):
        block = slice(r * rows, (r + 1) * rows)
        attended[block, :] = dot(weight_ref[block, :], value_ref[r])
    own_weights = jnp.where(own_place, own_weight * inverse, 0.0).astype(bf16)
    result = (attended[...] + dot(own_weights, new_value_ref[...])).astype(bf16)

    row = iota((total, total), 0)
    wanted = (row % requests) * rows + ((row // requests) % steps) * heads + row // pairs
    by_head = dot(one_hot(wanted, (total, total)), result).astype(bf16)
    for h in range(heads):
        home_ref[:, h * width : (h + 1) * width] = by_head[h * pairs : (h + 1) * pairs]
    home_ref[:, features : features + width] = new_value_ref[...]
    row = iota((total, 1), 0)
    lane = iota((total, lanes), 1)
    pieces = jnp.zeros((total, lanes), f32)
    for j in range(steps - 1):
        rest = by_step[j] - log_mass
        for piece in range(3):
            part = rest.astype(bf16).astype(f32)
            rest = rest - part
            target = (piece * (steps - 1) + j) * heads + row % heads
            pieces = jnp.where(lane == target, part, pieces)
    column = iota((pairs, total), 1)
    wanted = ((column // heads) % steps) * requests + column // rows
    gather = (wanted == iota((pairs, total), 0)).astype(f32).astype(bf16)
    scalars = scalars + dot(gather, pieces.astype(bf16))
    home_ref[:, features + width :] = scalars.astype(bf16)
    slots = send_ref.shape[0]
    pick = (iota((slots, pairs), 0) == flat_lanes).astype(f32).astype(bf16)
    block = features + width
    picked = dot(pick, home_ref[...])
    spread = (iota((slots, 8), 0) % 8 == iota((slots, 8), 1)).astype(f32).astype(bf16)
    send_ref[:, 0:block] = picked[:, 0:block].astype(bf16)
    integers = dot(spread, shared.astype(bf16))
    send_ref[:, block:] = (picked[:, block:] + integers).astype(bf16)
    copies[11].wait()


def combine_kernel(
    steps,
    heads,
    width,
    threshold,
    got_ref,
    home_ref,
    down_ref,
    weight_ref,
    weight_in,
    low_ref,
    theirs_ref,
    others_ref,
    final_ref,
    late_ref,
    rows_ref,
    sem,
):
    early = weight_ref.shape[0]
    copy = pltpu.make_async_copy(weight_in.at[pl.ds(early, late_ref.shape[0])], late_ref, sem)
    copy.start()
    slots, pairs = got_ref.shape[0], home_ref.shape[0]
    features = heads * width
    sent = features + width + lanes
    count = slots + pairs
    block = features + width
    requests = pairs // steps
    everyone = requests * (slots // 8)
    column = iota((lanes, everyone), 1)
    tile = (iota((lanes, everyone), 0) == lanes // 2 + column % requests).astype(f32).astype(bf16)
    column = iota((slots, everyone), 1)
    from_row = column // requests == iota((slots, everyone), 0) // 8
    tiled = jnp.where(from_row, dot(got_ref[:, block:], tile), 0.0).astype(bf16)
    kind = (iota((8, slots), 1) % 8 == iota((8, slots), 0)).astype(f32).astype(bf16)
    shared = dot(kind, tiled)
    tenants = shared[0:1] * 16.0 + shared[1:2]
    charge_rows = []
    for s in range(steps - 1):
        charge = shared[2:3] + (s + 1.0)
        upper = jnp.floor(charge * (1.0 / 16.0))
        admitted = shared[3 + s : 4 + s]
        charge_rows += [upper * admitted, (charge - upper * 16.0) * admitted]
    charge_rows += [jnp.zeros_like(tenants)] * (8 - len(charge_rows))
    charges = jnp.concatenate(charge_rows, axis=0).astype(bf16)

    scalars = jnp.concatenate(
        [got_ref[:, block:sent].astype(f32), home_ref[:, block:sent].astype(f32)], axis=0
    )
    first = 3 * heads * (steps - 1)
    tenant = scalars[:, first + 1 : first + 2] * 16.0 + scalars[:, first + 2 : first + 3]
    tokens = scalars[:, first + 3 : first + 4] * 32.0 + scalars[:, first + 4 : first + 5]
    same = (tenant == tenants).astype(f32).astype(bf16)
    grows = dot_t(same, charges)
    row = iota((count, 1), 0)
    step_of_row = jnp.where(row < slots, row % steps, (row - slots) // requests)
    served_now = jnp.zeros((count, 1), f32)
    served = []
    for s in range(steps):
        open_now = (tokens < threshold).astype(f32)
        flag = open_now * scalars[:, first + 5 + s : first + 6 + s]
        served.append(flag)
        served_now = jnp.where(step_of_row == s, flag, served_now)
        if s + 1 < steps:
            grow = grows[:, 2 * s : 2 * s + 1] * 16.0 + grows[:, 2 * s + 1 : 2 * s + 2]
            tokens = tokens + open_now * grow

    span = heads * (steps - 1)
    logs = scalars[:, 0:span] + scalars[:, span : 2 * span] + scalars[:, 2 * span : 3 * span]
    shown = [(served[j] > 0.5) & (step_of_row > j) for j in range(steps - 1)]
    by_step = [
        jnp.where(shown[j], logs[:, j * heads : (j + 1) * heads], -jnp.inf)
        for j in range(steps - 1)
    ]
    top = jnp.zeros((count, heads), f32)
    for j in range(steps - 1):
        top = jnp.maximum(top, by_step[j])
    old = jnp.exp(-top)
    new = [jnp.exp(by_step[j] - top) for j in range(steps - 1)]
    mass = old
    for j in range(steps - 1):
        mass = mass + new[j]
    inverse = served_now / mass
    old = old * inverse
    new = [weight * inverse for weight in new]
    values = jnp.concatenate(
        [got_ref[:, features:block], home_ref[:, features:block]], axis=0
    )
    first_row = jnp.where(row < slots, row - row % steps, slots + (row - slots) % requests)
    stride = jnp.where(row < slots, 1, requests)
    new_values = [
        dot(one_hot(first_row + stride * j, (count, count)), values) for j in range(steps - 1)
    ]
    for h in range(heads):
        part = slice(h * width, (h + 1) * width)
        rows = jnp.concatenate([got_ref[:, part], home_ref[:, part]], axis=0).astype(f32)
        rows = rows * old[:, h : h + 1]
        for j in range(steps - 1):
            rows = rows + new_values[j] * new[j][:, h : h + 1]
        rows = rows.astype(bf16)
        rows_ref[:, part] = rows[0:slots]
        final_ref[:, part] = rows[slots:]

    rank = down_ref.shape[1]
    every = down_ref.shape[0] * rank
    product = dot_t(rows_ref[...], down_ref[...].reshape(every, features))
    owner = (iota(product.shape, 1) // rank).astype(f32)
    product = jnp.where(owner == scalars[0:slots, first : first + 1], product, 0.0)
    folded = product[:, 0:lanes]
    for start in range(lanes, every, lanes):
        folded = folded + product[:, start : start + lanes]
    folded = folded + pltpu.roll(folded, rank, 1)
    half = slots // 2
    low_half = iota((half, lanes), 1) < rank
    low = jnp.where(low_half, folded[0:half], folded[half:])
    low_ref[...] = low
    copy.wait()
    for index, product in enumerate(project(1, first_blocks, final_ref, weight_ref, late_ref)):
        theirs_ref[:, index * features : (index + 1) * features] = product.astype(bf16)
    start = len(first_blocks) * features
    upper = low.astype(bf16)
    theirs_ref[:, start : start + lanes] = upper
    theirs_ref[:, start + lanes :] = (low - upper.astype(f32)).astype(bf16)
    for index, product in enumerate(project(1, other_blocks, final_ref, weight_ref, late_ref)):
        others_ref[index] = product.astype(bf16)


def project(flip, wanted, rows_ref, weight_ref, late_ref):
    parts = lax.axis_size("z")
    width = weight_ref.shape[1] // (2 * parts)
    early = weight_ref.shape[0]
    core = lax.axis_index("core")
    mine = core if flip == 0 else 1 - core
    here = lax.axis_index("z")
    way = 1 - 2 * lax.rem(here, 2)
    products = []
    for part in wanted:
        target = lax.rem(here + way * part + parts, parts)
        start = pl.multiple_of((2 * target + mine) * width, width)
        block = pl.ds(start, width)
        product = dot(rows_ref[:, 0:early], weight_ref[:, block])
        products.append(product + dot(rows_ref[:, early:], late_ref[:, block]))
    return products


def ours_kernel(rows_ref, weight_ref, late_ref, out_ref):
    blocks = first_blocks + other_blocks
    for index, product in enumerate(project(0, blocks, rows_ref, weight_ref, late_ref)):
        out_ref[index] = product


def mix_kernel(low_ref, ours_ref, came_ref, others_ref, low_out, first_out, others_out):
    count, _, width = first_out.shape
    start = count * width
    other = came_ref[:, start : start + lanes].astype(f32)
    other = other + came_ref[:, start + lanes :].astype(f32)
    low = (low_ref[...] + other).astype(bf16)
    for part in range(low_out.shape[0]):
        low_out[part] = low
    for index in range(count):
        came = came_ref[:, index * width : (index + 1) * width].astype(f32)
        first_out[index] = (ours_ref[index] + came).astype(bf16)
    others_out[...] = others_ref[...]


def hop_kernel(first, ours_ref, others_ref, came_ref, out_ref):
    skip = len(first_blocks) + first
    for index in range(out_ref.shape[0]):
        here = ours_ref[skip + index] + others_ref[first + index].astype(f32)
        out_ref[index] = (came_ref[index].astype(f32) + here).astype(bf16)


def late_hop_kernel(first, ours_ref, others_ref, came_ref, after_ref, out_ref):
    hop_kernel(first, ours_ref, others_ref, came_ref, out_ref)


def up_kernel(first_scalar, parts_ref, held_ref, up_ref, out_ref):
    rank = up_ref.shape[1]
    every = up_ref.shape[0] * rank
    low = parts_ref[0].astype(f32)
    for part in range(1, parts_ref.shape[0]):
        low = low + parts_ref[part].astype(f32)
    other = pltpu.roll(low, rank, 1)
    first = iota(low.shape, 1) < rank
    low = jnp.concatenate(
        [jnp.where(first, low, other), jnp.where(first, other, low)], axis=0
    )
    wide = jnp.concatenate([low] * (every // lanes), axis=1)
    owner = (iota(wide.shape, 1) // rank).astype(f32)
    held = held_ref[:, first_scalar : first_scalar + 1].astype(f32)
    wide = jnp.where(owner == held, wide, 0.0).astype(bf16)
    out_ref[...] = dot(wide, up_ref[...].reshape(every, up_ref.shape[2])).astype(bf16)


def finish_kernel(ours_ref, others_ref, first_ref, second_ref, back_ref, term_ref, out_ref):
    total = ours_ref[0] + others_ref[0].astype(f32)
    total = total + first_ref[0].astype(f32) + second_ref[0].astype(f32)
    term = dot(back_ref[...], term_ref[...])
    out_ref[...] = (total + adapter_scale * term).astype(bf16)


def per_device(
    queries,
    cache_keys,
    cache_values,
    new_keys,
    new_values,
    lengths,
    admitted,
    request_tenant,
    tenant_adapter,
    adapter_slot,
    tenant_tokens,
    out_weight,
    adapter_down_factor,
    adapter_up_factor,
):
    holders = lax.axis_size("batch")
    parts = lax.axis_size("z")
    steps, requests, features = queries.shape
    context, width = cache_keys.shape[1], cache_keys.shape[3]
    heads = features // width
    rows = steps * heads
    total = requests * rows
    pairs = steps * requests
    adapters_held, rank, _ = adapter_down_factor.shape
    every = adapters_held * rank
    threshold = float(3 * context)
    early = features * 4 // 8
    slots = holders * capacity * steps
    first_scalar = 3 * heads * (steps - 1)
    sent = features + width + lanes
    shape = jax.ShapeDtypeStruct

    home, send, back, weight = call(
        functools.partial(attend_kernel, steps, requests, heads, adapters_held),
        (
            shape((pairs, sent), bf16),
            shape((slots, sent), bf16),
            shape((pairs, slots), bf16),
            pltpu.VMEM((early, out_weight.shape[1]), bf16),
        ),
        [HBM] * 12,
        (VMEM,) * 4,
        4 * total * context * width,
        4 * cache_keys.size,
        [
            pltpu.SMEM((requests,), jnp.int32),
            pltpu.SMEM((requests,), jnp.int32),
            pltpu.SMEM((steps, requests), jnp.int32),
            pltpu.SMEM(tenant_adapter.shape, jnp.int32),
            pltpu.SMEM(adapter_slot.shape, jnp.int32),
            pltpu.SMEM(tenant_tokens.shape, jnp.int32),
            pltpu.SMEM((holders,), jnp.int32),
            pltpu.VMEM((pairs, features), bf16),
            pltpu.VMEM((requests, context, width), bf16),
            pltpu.VMEM((requests, context, width), bf16),
            pltpu.VMEM((pairs, width), bf16),
            pltpu.VMEM((pairs, width), bf16),
            pltpu.VMEM((total, width), f32),
            pltpu.VMEM((total, context), f32),
            pltpu.VMEM((total, context), bf16),
            pltpu.SemaphoreType.DMA((12,)),
        ],
        40 << 20,
    )(
        *map(
            in_hbm,
            (
                request_tenant,
                lengths,
                admitted,
                tenant_adapter,
                adapter_slot,
                tenant_tokens,
                queries.reshape(pairs, features),
                cache_keys.reshape(requests, context, width),
                cache_values.reshape(requests, context, width),
                new_keys.reshape(pairs, width),
                new_values.reshape(pairs, width),
                out_weight,
            ),
        )
    )
    got = lax.all_to_all(send, "batch", split_axis=0, concat_axis=0, tiled=True)
    weight = in_vmem(weight)
    two = shape((2, pairs, features), bf16)
    one = shape((1, pairs, features), bf16)
    six = shape((len(other_blocks), pairs, features), bf16)
    blocks = shape((parts, pairs, features), f32)
    low, theirs, others, final, late = call(
        functools.partial(combine_kernel, steps, heads, width, threshold),
        (
            shape((slots // 2, lanes), f32),
            shape((pairs, 2 * features + 2 * lanes), bf16),
            six,
            shape((pairs, features), bf16),
            pltpu.VMEM((features - early, out_weight.shape[1]), bf16),
        ),
        [VMEM] * 4 + [HBM],
        (VMEM,) * 5,
        2 * slots * features * every,
        out_weight.size,
        [pltpu.VMEM((slots, features), bf16), pltpu.SemaphoreType.DMA],
    )(got, home, adapter_down_factor, weight, in_hbm(out_weight))
    swap = [(0, 1), (1, 0)]
    theirs = lax.ppermute(theirs, "core", swap)
    ours = call(
        ours_kernel,
        blocks,
        [VMEM] * 3,
        VMEM,
        pairs * out_weight.size,
        out_weight.size,
    )(final, weight, in_vmem(late))
    low, sums, others = call(
        mix_kernel,
        (shape((parts, slots // 2, lanes), bf16), two, six),
        [VMEM] * 4,
        (VMEM,) * 3,
        2 * two.size,
        8 * two.size,
    )(low, ours, theirs, others)
    others = lax.ppermute(others, "core", swap)
    low = lax.all_to_all(low, "z", split_axis=0, concat_axis=0, tiled=True)

    def hop(kernel, first, out, *args):
        return call(
            functools.partial(kernel, first),
            out,
            [VMEM] * 3 + [HBM] * (len(args) - 3),
            VMEM,
            out.size,
            6 * out.size,
        )(*args)

    odd = [(i, i + 1 - 2 * (i % 2)) for i in range(parts)]
    even = [(i, (i - 1 + 2 * (i % 2)) % parts) for i in range(parts)]
    sums = lax.ppermute(sums, "z", odd)
    sums = lax.ppermute(hop(hop_kernel, 0, two, ours, others, sums), "z", even)
    term = call(
        functools.partial(up_kernel, first_scalar),
        shape((slots, features), bf16),
        [VMEM] * 3,
        VMEM,
        2 * slots * features * every,
        4 * slots * features,
    )(low, got[:, features + width : sent], adapter_up_factor)
    sums = hop(late_hop_kernel, 2, two, ours, others, sums, term)
    sums = lax.ppermute(sums, "z", odd)
    last = lax.ppermute(hop(hop_kernel, 4, one, ours, others, sums), "z", even)
    term = lax.all_to_all(term, "batch", split_axis=0, concat_axis=0, tiled=True)
    out = call(
        finish_kernel,
        shape((pairs, features), bf16),
        [VMEM] * 6,
        VMEM,
        2 * pairs * slots * features,
        10 * one.size,
    )(ours[-1:], others[-1:], sums[1:], last, back, term)
    return out.reshape(steps, requests, features)


def solution(mesh):
    batch, tensor = mesh.shape["batch"], mesh.shape["tensor"]
    split = Mesh(mesh.devices.reshape(batch, tensor // 2, 2), ("batch", "z", "core"))
    tensor_axes = ("z", "core")
    placed = (
        P(None, "batch", tensor_axes),
        P("batch", None, tensor_axes, None),
        P("batch", None, tensor_axes, None),
        P(None, "batch", tensor_axes, None),
        P(None, "batch", tensor_axes, None),
        P("batch"),
        P(None, "batch"),
        P("batch"),
        P(),
        P(),
        P(),
        P(tensor_axes, None),
        P("batch", None, tensor_axes),
        P("batch", None, tensor_axes),
    )
    return jax.shard_map(
        per_device,
        mesh=split,
        in_specs=placed,
        out_specs=P(None, "batch", tensor_axes),
        check_vma=False,
    )
```

```python
import functools

import jax
import jax.numpy as jnp
from jax import lax
from jax.experimental import pallas as pl
from jax.experimental.pallas import tpu as pltpu
from jax.sharding import Mesh
from jax.sharding import PartitionSpec as P

adapter_scale = 2.0
capacity = 2
lanes = 128
first_blocks = (4, 3)
other_blocks = (5, 6, 2, 1, 7, 0)
f32 = jnp.float32
bf16 = jnp.bfloat16
VMEM = pl.BlockSpec(memory_space=pltpu.VMEM)
SMEM = pl.BlockSpec(memory_space=pltpu.SMEM)
HBM = pl.BlockSpec(memory_space=pltpu.HBM)


def in_hbm(array):
    return pltpu.with_memory_space_constraint(array, pltpu.HBM)


def in_vmem(array):
    return pltpu.with_memory_space_constraint(array, pltpu.VMEM)


def iota(shape, axis):
    return lax.broadcasted_iota(jnp.int32, shape, axis)


def dot(a, b):
    return jnp.dot(a, b, preferred_element_type=f32)


def dot_t(a, b):
    return lax.dot_general(a, b, (((1,), (1,)), ((), ())), preferred_element_type=f32)


def call(kernel, out_shape, in_specs, out_specs, flops, moved, scratch=(), limit=16 << 20):
    return pl.pallas_call(
        kernel,
        out_shape=out_shape,
        in_specs=in_specs,
        out_specs=out_specs,
        scratch_shapes=list(scratch),
        cost_estimate=pl.CostEstimate(flops=flops, bytes_accessed=moved, transcendentals=0),
        compiler_params=pltpu.CompilerParams(vmem_limit_bytes=limit),
    )


def fetch_all(pairs, sems):
    copies = []
    for index, (source, target) in enumerate(pairs):
        copy = pltpu.make_async_copy(source, target, sems.at[index])
        copy.start()
        copies.append(copy)
    return copies


def one_hot(wanted, shape):
    return (wanted == iota(shape, 1)).astype(f32).astype(bf16)


def attend_kernel(
    steps,
    requests,
    heads,
    adapters_held,
    tenant_in,
    length_in,
    admitted_in,
    tenant_adapter_in,
    adapter_slot_in,
    token_in,
    query_in,
    key_in,
    value_in,
    new_key_in,
    new_value_in,
    projection_in,
    home_ref,
    send_ref,
    back_ref,
    projection_ref,
    tenant_ref,
    length_ref,
    admitted_ref,
    tenant_adapter_ref,
    adapter_slot_ref,
    token_ref,
    seen,
    query_ref,
    key_ref,
    value_ref,
    new_key_ref,
    new_value_ref,
    attended,
    score_ref,
    weight_ref,
    sems,
):
    rows = steps * heads
    total = requests * rows
    pairs = steps * requests
    width = key_ref.shape[2]
    context = key_ref.shape[1]
    features = heads * width
    scale = width ** (-0.5)
    copies = fetch_all(
        [
            (tenant_in, tenant_ref),
            (length_in, length_ref),
            (admitted_in, admitted_ref),
            (tenant_adapter_in, tenant_adapter_ref),
            (adapter_slot_in, adapter_slot_ref),
            (token_in, token_ref),
            (query_in, query_ref),
            (new_key_in, new_key_ref),
            (new_value_in, new_value_ref),
            (key_in, key_ref),
            (value_in, value_ref),
            (projection_in.at[pl.ds(0, projection_ref.shape[0])], projection_ref),
        ],
        sems,
    )
    for index in range(seen.shape[0]):
        seen[index] = 0
    for copy in copies[:9]:
        copy.wait()

    lane = iota((1, lanes), 1)
    place = iota((pairs, 1), 0)
    lane_of_pair = iota((1, pairs), 1)
    shared_row = iota((8, lanes), 0)
    shared_lane = iota((8, lanes), 1)
    flat_rows = jnp.zeros((pairs, 1), jnp.int32)
    flat_lanes = jnp.zeros((1, pairs), jnp.int32)
    scalars = jnp.zeros((pairs, lanes), f32)
    shared = jnp.zeros((8, lanes), f32)
    first_scalar = 3 * heads * (steps - 1)
    for r in range(requests):
        tenant = tenant_ref[r]
        tokens = token_ref[tenant]
        slot = adapter_slot_ref[tenant_adapter_ref[tenant]]
        holder = slot // adapters_held
        position = seen[holder]
        seen[holder] = position + 1
        flat = (holder * capacity + position) * steps
        flat_rows = jnp.where(place % requests == r, flat, flat_rows)
        flat_lanes = jnp.where(lane_of_pair % requests == r, flat, flat_lanes)
        tenant_parts = [tenant // 16, tenant % 16]
        admits = [admitted_ref[s, r] for s in range(steps)]
        own = [slot - holder * adapters_held] + tenant_parts + [tokens // 32, tokens % 32] + admits
        line = jnp.zeros((1, lanes), jnp.int32)
        for index, value in enumerate(own):
            line = jnp.where(lane == first_scalar + index, value, line)
        scalars = jnp.where(place % requests == r, line.astype(f32), scalars)
        column = jnp.zeros((8, lanes), jnp.int32)
        for index, value in enumerate(tenant_parts + [length_ref[r]] + admits):
            column = jnp.where(shared_row == index, value, column)
        shared = jnp.where(shared_lane == lanes // 2 + r, column.astype(f32), shared)
    flat_rows = flat_rows + place // requests
    flat_lanes = flat_lanes + lane_of_pair // requests
    back_ref[...] = one_hot(flat_rows, back_ref.shape)

    by_head = jnp.concatenate(
        [query_ref[:, h * width : (h + 1) * width] for h in range(heads)], axis=0
    )
    row = iota((total, total), 0)
    wanted = (row % heads) * pairs + ((row // heads) % steps) * requests + row // rows
    by_request = dot(one_hot(wanted, (total, total)), by_head).astype(bf16)
    new_scores = dot_t(by_request, new_key_ref[...]) * scale
    row = iota((total, 1), 0)
    new_column = iota((total, pairs), 1)
    by_step = [
        jnp.sum(
            jnp.where(new_column == j * requests + row // rows, new_scores, 0.0),
            axis=1,
            keepdims=True,
        )
        for j in range(steps)
    ]
    step_of_row = (row // heads) % steps
    own_score = by_step[0]
    for s in range(1, steps):
        own_score = jnp.where(step_of_row == s, by_step[s], own_score)
    own_place = new_column == step_of_row * requests + row // rows
    position = iota((rows, context), 1)
    copies[9].wait()
    for r in range(requests):
        block = slice(r * rows, (r + 1) * rows)
        scores = dot_t(by_request[block], key_ref[r]) * scale
        score_ref[block, :] = jnp.where(position < length_ref[r], scores, -jnp.inf)
    scores = score_ref[...]
    top = jnp.maximum(jnp.max(scores, axis=1, keepdims=True), own_score)
    weight = jnp.exp(scores - top)
    own_weight = jnp.exp(own_score - top)
    mass = jnp.sum(weight, axis=1, keepdims=True) + own_weight
    inverse = 1.0 / mass
    log_mass = top + jnp.log(mass)
    weight_ref[...] = (weight * inverse).astype(bf16)
    copies[10].wait()
    for r in range(requests):
        block = slice(r * rows, (r + 1) * rows)
        attended[block, :] = dot(weight_ref[block, :], value_ref[r])
    own_weights = jnp.where(own_place, own_weight * inverse, 0.0).astype(bf16)
    result = (attended[...] + dot(own_weights, new_value_ref[...])).astype(bf16)

    row = iota((total, total), 0)
    wanted = (row % requests) * rows + ((row // requests) % steps) * heads + row // pairs
    by_head = dot(one_hot(wanted, (total, total)), result).astype(bf16)
    for h in range(heads):
        home_ref[:, h * width : (h + 1) * width] = by_head[h * pairs : (h + 1) * pairs]
    home_ref[:, features : features + width] = new_value_ref[...]
    row = iota((total, 1), 0)
    lane = iota((total, lanes), 1)
    pieces = jnp.zeros((total, lanes), f32)
    for j in range(steps - 1):
        rest = by_step[j] - log_mass
        for piece in range(3):
            part = rest.astype(bf16).astype(f32)
            rest = rest - part
            target = (piece * (steps - 1) + j) * heads + row % heads
            pieces = jnp.where(lane == target, part, pieces)
    column = iota((pairs, total), 1)
    wanted = ((column // heads) % steps) * requests + column // rows
    gather = (wanted == iota((pairs, total), 0)).astype(f32).astype(bf16)
    scalars = scalars + dot(gather, pieces.astype(bf16))
    home_ref[:, features + width :] = scalars.astype(bf16)
    slots = send_ref.shape[0]
    pick = (iota((slots, pairs), 0) == flat_lanes).astype(f32).astype(bf16)
    block = features + width
    picked = dot(pick, home_ref[...])
    spread = (iota((slots, 8), 0) % 8 == iota((slots, 8), 1)).astype(f32).astype(bf16)
    send_ref[:, 0:block] = picked[:, 0:block].astype(bf16)
    integers = dot(spread, shared.astype(bf16))
    send_ref[:, block:] = (picked[:, block:] + integers).astype(bf16)
    copies[11].wait()


def combine_kernel(
    steps,
    heads,
    width,
    threshold,
    got_ref,
    home_ref,
    down_ref,
    weight_ref,
    weight_in,
    low_ref,
    theirs_ref,
    others_ref,
    final_ref,
    late_ref,
    rows_ref,
    sem,
):
    early = weight_ref.shape[0]
    copy = pltpu.make_async_copy(weight_in.at[pl.ds(early, late_ref.shape[0])], late_ref, sem)
    copy.start()
    slots, pairs = got_ref.shape[0], home_ref.shape[0]
    features = heads * width
    sent = features + width + lanes
    count = slots + pairs
    block = features + width
    requests = pairs // steps
    everyone = requests * (slots // 8)
    column = iota((lanes, everyone), 1)
    tile = (iota((lanes, everyone), 0) == lanes // 2 + column % requests).astype(f32).astype(bf16)
    column = iota((slots, everyone), 1)
    from_row = column // requests == iota((slots, everyone), 0) // 8
    tiled = jnp.where(from_row, dot(got_ref[:, block:], tile), 0.0).astype(bf16)
    kind = (iota((8, slots), 1) % 8 == iota((8, slots), 0)).astype(f32).astype(bf16)
    shared = dot(kind, tiled)
    tenants = shared[0:1] * 16.0 + shared[1:2]
    charge_rows = []
    for s in range(steps - 1):
        charge = shared[2:3] + (s + 1.0)
        upper = jnp.floor(charge * (1.0 / 16.0))
        admitted = shared[3 + s : 4 + s]
        charge_rows += [upper * admitted, (charge - upper * 16.0) * admitted]
    charge_rows += [jnp.zeros_like(tenants)] * (8 - len(charge_rows))
    charges = jnp.concatenate(charge_rows, axis=0).astype(bf16)

    scalars = jnp.concatenate(
        [got_ref[:, block:sent].astype(f32), home_ref[:, block:sent].astype(f32)], axis=0
    )
    first = 3 * heads * (steps - 1)
    tenant = scalars[:, first + 1 : first + 2] * 16.0 + scalars[:, first + 2 : first + 3]
    tokens = scalars[:, first + 3 : first + 4] * 32.0 + scalars[:, first + 4 : first + 5]
    same = (tenant == tenants).astype(f32).astype(bf16)
    grows = dot_t(same, charges)
    row = iota((count, 1), 0)
    step_of_row = jnp.where(row < slots, row % steps, (row - slots) // requests)
    served_now = jnp.zeros((count, 1), f32)
    served = []
    for s in range(steps):
        open_now = (tokens < threshold).astype(f32)
        flag = open_now * scalars[:, first + 5 + s : first + 6 + s]
        served.append(flag)
        served_now = jnp.where(step_of_row == s, flag, served_now)
        if s + 1 < steps:
            grow = grows[:, 2 * s : 2 * s + 1] * 16.0 + grows[:, 2 * s + 1 : 2 * s + 2]
            tokens = tokens + open_now * grow

    span = heads * (steps - 1)
    logs = scalars[:, 0:span] + scalars[:, span : 2 * span] + scalars[:, 2 * span : 3 * span]
    shown = [(served[j] > 0.5) & (step_of_row > j) for j in range(steps - 1)]
    by_step = [
        jnp.where(shown[j], logs[:, j * heads : (j + 1) * heads], -jnp.inf)
        for j in range(steps - 1)
    ]
    top = jnp.zeros((count, heads), f32)
    for j in range(steps - 1):
        top = jnp.maximum(top, by_step[j])
    old = jnp.exp(-top)
    new = [jnp.exp(by_step[j] - top) for j in range(steps - 1)]
    mass = old
    for j in range(steps - 1):
        mass = mass + new[j]
    inverse = served_now / mass
    old = old * inverse
    new = [weight * inverse for weight in new]
    values = jnp.concatenate(
        [got_ref[:, features:block], home_ref[:, features:block]], axis=0
    )
    first_row = jnp.where(row < slots, row - row % steps, slots + (row - slots) % requests)
    stride = jnp.where(row < slots, 1, requests)
    new_values = [
        dot(one_hot(first_row + stride * j, (count, count)), values) for j in range(steps - 1)
    ]
    for h in range(heads):
        part = slice(h * width, (h + 1) * width)
        rows = jnp.concatenate([got_ref[:, part], home_ref[:, part]], axis=0).astype(f32)
        rows = rows * old[:, h : h + 1]
        for j in range(steps - 1):
            rows = rows + new_values[j] * new[j][:, h : h + 1]
        rows = rows.astype(bf16)
        rows_ref[:, part] = rows[0:slots]
        final_ref[:, part] = rows[slots:]

    rank = down_ref.shape[1]
    every = down_ref.shape[0] * rank
    product = dot_t(rows_ref[...], down_ref[...].reshape(every, features))
    owner = (iota(product.shape, 1) // rank).astype(f32)
    product = jnp.where(owner == scalars[0:slots, first : first + 1], product, 0.0)
    folded = product[:, 0:lanes]
    for start in range(lanes, every, lanes):
        folded = folded + product[:, start : start + lanes]
    folded = folded + pltpu.roll(folded, rank, 1)
    half = slots // 2
    low_half = iota((half, lanes), 1) < rank
    low = jnp.where(low_half, folded[0:half], folded[half:])
    low_ref[...] = low
    copy.wait()
    for index, product in enumerate(project(1, first_blocks, final_ref, weight_ref, late_ref)):
        theirs_ref[:, index * features : (index + 1) * features] = product.astype(bf16)
    start = len(first_blocks) * features
    upper = low.astype(bf16)
    theirs_ref[:, start : start + lanes] = upper
    theirs_ref[:, start + lanes :] = (low - upper.astype(f32)).astype(bf16)
    for index, product in enumerate(project(1, other_blocks[:1], final_ref, weight_ref, late_ref)):
        others_ref[index] = product.astype(bf16)


def project(flip, wanted, rows_ref, weight_ref, late_ref):
    parts = lax.axis_size("z")
    width = weight_ref.shape[1] // (2 * parts)
    early = weight_ref.shape[0]
    core = lax.axis_index("core")
    mine = core if flip == 0 else 1 - core
    here = lax.axis_index("z")
    way = 1 - 2 * lax.rem(here, 2)
    products = []
    for part in wanted:
        target = lax.rem(here + way * part + parts, parts)
        start = pl.multiple_of((2 * target + mine) * width, width)
        block = pl.ds(start, width)
        product = dot(rows_ref[:, 0:early], weight_ref[:, block])
        products.append(product + dot(rows_ref[:, early:], late_ref[:, block]))
    return products


def rest_kernel(rows_ref, weight_ref, late_ref, out_ref, others_ref):
    blocks = first_blocks + other_blocks
    for index, product in enumerate(project(0, blocks, rows_ref, weight_ref, late_ref)):
        out_ref[index] = product
    for index, product in enumerate(project(1, other_blocks[1:], rows_ref, weight_ref, late_ref)):
        others_ref[index] = product.astype(bf16)


def mix_kernel(low_ref, ours_ref, came_ref, next_ref, others_ref, low_out, first_out, others_out):
    count, _, width = first_out.shape
    start = count * width
    other = came_ref[:, start : start + lanes].astype(f32)
    other = other + came_ref[:, start + lanes :].astype(f32)
    low = (low_ref[...] + other).astype(bf16)
    for part in range(low_out.shape[0]):
        low_out[part] = low
    for index in range(count):
        came = came_ref[:, index * width : (index + 1) * width].astype(f32)
        first_out[index] = (ours_ref[index] + came).astype(bf16)
    others_out[0:1] = next_ref[...]
    others_out[1:] = others_ref[...]


def hop_kernel(first, ours_ref, others_ref, came_ref, out_ref):
    skip = len(first_blocks) + first
    for index in range(out_ref.shape[0]):
        here = ours_ref[skip + index] + others_ref[first + index].astype(f32)
        out_ref[index] = (came_ref[index].astype(f32) + here).astype(bf16)


def late_hop_kernel(first, ours_ref, others_ref, came_ref, after_ref, out_ref):
    hop_kernel(first, ours_ref, others_ref, came_ref, out_ref)


def up_kernel(first_scalar, parts_ref, held_ref, up_ref, out_ref):
    rank = up_ref.shape[1]
    every = up_ref.shape[0] * rank
    low = parts_ref[0].astype(f32)
    for part in range(1, parts_ref.shape[0]):
        low = low + parts_ref[part].astype(f32)
    other = pltpu.roll(low, rank, 1)
    first = iota(low.shape, 1) < rank
    low = jnp.concatenate(
        [jnp.where(first, low, other), jnp.where(first, other, low)], axis=0
    )
    wide = jnp.concatenate([low] * (every // lanes), axis=1)
    owner = (iota(wide.shape, 1) // rank).astype(f32)
    held = held_ref[:, first_scalar : first_scalar + 1].astype(f32)
    wide = jnp.where(owner == held, wide, 0.0).astype(bf16)
    out_ref[...] = dot(wide, up_ref[...].reshape(every, up_ref.shape[2])).astype(bf16)


def finish_kernel(ours_ref, others_ref, first_ref, second_ref, back_ref, term_ref, out_ref):
    total = ours_ref[0] + others_ref[0].astype(f32)
    total = total + first_ref[0].astype(f32) + second_ref[0].astype(f32)
    term = dot(back_ref[...], term_ref[...])
    out_ref[...] = (total + adapter_scale * term).astype(bf16)


def per_device(
    queries,
    cache_keys,
    cache_values,
    new_keys,
    new_values,
    lengths,
    admitted,
    request_tenant,
    tenant_adapter,
    adapter_slot,
    tenant_tokens,
    out_weight,
    adapter_down_factor,
    adapter_up_factor,
):
    holders = lax.axis_size("batch")
    parts = lax.axis_size("z")
    steps, requests, features = queries.shape
    context, width = cache_keys.shape[1], cache_keys.shape[3]
    heads = features // width
    rows = steps * heads
    total = requests * rows
    pairs = steps * requests
    adapters_held, rank, _ = adapter_down_factor.shape
    every = adapters_held * rank
    threshold = float(3 * context)
    early = features * 4 // 8
    slots = holders * capacity * steps
    first_scalar = 3 * heads * (steps - 1)
    sent = features + width + lanes
    shape = jax.ShapeDtypeStruct

    home, send, back, weight = call(
        functools.partial(attend_kernel, steps, requests, heads, adapters_held),
        (
            shape((pairs, sent), bf16),
            shape((slots, sent), bf16),
            shape((pairs, slots), bf16),
            pltpu.VMEM((early, out_weight.shape[1]), bf16),
        ),
        [HBM] * 12,
        (VMEM,) * 4,
        4 * total * context * width,
        4 * cache_keys.size,
        [
            pltpu.SMEM((requests,), jnp.int32),
            pltpu.SMEM((requests,), jnp.int32),
            pltpu.SMEM((steps, requests), jnp.int32),
            pltpu.SMEM(tenant_adapter.shape, jnp.int32),
            pltpu.SMEM(adapter_slot.shape, jnp.int32),
            pltpu.SMEM(tenant_tokens.shape, jnp.int32),
            pltpu.SMEM((holders,), jnp.int32),
            pltpu.VMEM((pairs, features), bf16),
            pltpu.VMEM((requests, context, width), bf16),
            pltpu.VMEM((requests, context, width), bf16),
            pltpu.VMEM((pairs, width), bf16),
            pltpu.VMEM((pairs, width), bf16),
            pltpu.VMEM((total, width), f32),
            pltpu.VMEM((total, context), f32),
            pltpu.VMEM((total, context), bf16),
            pltpu.SemaphoreType.DMA((12,)),
        ],
        40 << 20,
    )(
        *map(
            in_hbm,
            (
                request_tenant,
                lengths,
                admitted,
                tenant_adapter,
                adapter_slot,
                tenant_tokens,
                queries.reshape(pairs, features),
                cache_keys.reshape(requests, context, width),
                cache_values.reshape(requests, context, width),
                new_keys.reshape(pairs, width),
                new_values.reshape(pairs, width),
                out_weight,
            ),
        )
    )
    got = lax.all_to_all(send, "batch", split_axis=0, concat_axis=0, tiled=True)
    weight = in_vmem(weight)
    two = shape((2, pairs, features), bf16)
    one = shape((1, pairs, features), bf16)
    six = shape((len(other_blocks), pairs, features), bf16)
    blocks = shape((parts, pairs, features), f32)
    low, theirs, following, final, late = call(
        functools.partial(combine_kernel, steps, heads, width, threshold),
        (
            shape((slots // 2, lanes), f32),
            shape((pairs, 2 * features + 2 * lanes), bf16),
            one,
            shape((pairs, features), bf16),
            pltpu.VMEM((features - early, out_weight.shape[1]), bf16),
        ),
        [VMEM] * 4 + [HBM],
        (VMEM,) * 5,
        2 * slots * features * every,
        out_weight.size,
        [pltpu.VMEM((slots, features), bf16), pltpu.SemaphoreType.DMA],
    )(got, home, adapter_down_factor, weight, in_hbm(out_weight))
    swap = [(0, 1), (1, 0)]
    theirs = lax.ppermute(theirs, "core", swap)
    ours, others = call(
        rest_kernel,
        (blocks, shape((len(other_blocks) - 1, pairs, features), bf16)),
        [VMEM] * 3,
        (VMEM,) * 2,
        pairs * out_weight.size,
        out_weight.size,
    )(final, weight, in_vmem(late))
    low, sums, others = call(
        mix_kernel,
        (shape((parts, slots // 2, lanes), bf16), two, six),
        [VMEM] * 5,
        (VMEM,) * 3,
        2 * two.size,
        8 * two.size,
    )(low, ours, theirs, following, others)
    others = lax.ppermute(others, "core", swap)
    low = lax.all_to_all(low, "z", split_axis=0, concat_axis=0, tiled=True)

    def hop(kernel, first, out, *args):
        return call(
            functools.partial(kernel, first),
            out,
            [VMEM] * 3 + [HBM] * (len(args) - 3),
            VMEM,
            out.size,
            6 * out.size,
        )(*args)

    odd = [(i, i + 1 - 2 * (i % 2)) for i in range(parts)]
    even = [(i, (i - 1 + 2 * (i % 2)) % parts) for i in range(parts)]
    sums = lax.ppermute(sums, "z", odd)
    sums = lax.ppermute(hop(hop_kernel, 0, two, ours, others, sums), "z", even)
    term = call(
        functools.partial(up_kernel, first_scalar),
        shape((slots, features), bf16),
        [VMEM] * 3,
        VMEM,
        2 * slots * features * every,
        4 * slots * features,
    )(low, got[:, features + width : sent], adapter_up_factor)
    sums = hop(late_hop_kernel, 2, two, ours, others, sums, term)
    sums = lax.ppermute(sums, "z", odd)
    last = lax.ppermute(hop(hop_kernel, 4, one, ours, others, sums), "z", even)
    term = lax.all_to_all(term, "batch", split_axis=0, concat_axis=0, tiled=True)
    out = call(
        finish_kernel,
        shape((pairs, features), bf16),
        [VMEM] * 6,
        VMEM,
        2 * pairs * slots * features,
        10 * one.size,
    )(ours[-1:], others[-1:], sums[1:], last, back, term)
    return out.reshape(steps, requests, features)


def solution(mesh):
    batch, tensor = mesh.shape["batch"], mesh.shape["tensor"]
    split = Mesh(mesh.devices.reshape(batch, tensor // 2, 2), ("batch", "z", "core"))
    tensor_axes = ("z", "core")
    placed = (
        P(None, "batch", tensor_axes),
        P("batch", None, tensor_axes, None),
        P("batch", None, tensor_axes, None),
        P(None, "batch", tensor_axes, None),
        P(None, "batch", tensor_axes, None),
        P("batch"),
        P(None, "batch"),
        P("batch"),
        P(),
        P(),
        P(),
        P(tensor_axes, None),
        P("batch", None, tensor_axes),
        P("batch", None, tensor_axes),
    )
    return jax.shard_map(
        per_device,
        mesh=split,
        in_specs=placed,
        out_specs=P(None, "batch", tensor_axes),
        check_vma=False,
    )
```

```python
import functools

import jax
import jax.numpy as jnp
from jax import lax
from jax.experimental import pallas as pl
from jax.experimental.pallas import tpu as pltpu
from jax.sharding import Mesh
from jax.sharding import PartitionSpec as P

adapter_scale = 2.0
capacity = 2
lanes = 128
first_blocks = (4, 3)
other_blocks = (5, 6, 2, 1, 7, 0)
f32 = jnp.float32
bf16 = jnp.bfloat16
VMEM = pl.BlockSpec(memory_space=pltpu.VMEM)
SMEM = pl.BlockSpec(memory_space=pltpu.SMEM)
HBM = pl.BlockSpec(memory_space=pltpu.HBM)


def in_hbm(array):
    return pltpu.with_memory_space_constraint(array, pltpu.HBM)


def in_vmem(array):
    return pltpu.with_memory_space_constraint(array, pltpu.VMEM)


def iota(shape, axis):
    return lax.broadcasted_iota(jnp.int32, shape, axis)


def dot(a, b):
    return jnp.dot(a, b, preferred_element_type=f32)


def dot_t(a, b):
    return lax.dot_general(a, b, (((1,), (1,)), ((), ())), preferred_element_type=f32)


def call(kernel, out_shape, in_specs, out_specs, flops, moved, scratch=(), limit=16 << 20):
    return pl.pallas_call(
        kernel,
        out_shape=out_shape,
        in_specs=in_specs,
        out_specs=out_specs,
        scratch_shapes=list(scratch),
        cost_estimate=pl.CostEstimate(flops=flops, bytes_accessed=moved, transcendentals=0),
        compiler_params=pltpu.CompilerParams(vmem_limit_bytes=limit),
    )


def fetch_all(pairs, sems):
    copies = []
    for index, (source, target) in enumerate(pairs):
        copy = pltpu.make_async_copy(source, target, sems.at[index])
        copy.start()
        copies.append(copy)
    return copies


def one_hot(wanted, shape):
    return (wanted == iota(shape, 1)).astype(f32).astype(bf16)


def attend_kernel(
    steps,
    requests,
    heads,
    adapters_held,
    tenant_in,
    length_in,
    admitted_in,
    tenant_adapter_in,
    adapter_slot_in,
    token_in,
    query_in,
    key_in,
    value_in,
    new_key_in,
    new_value_in,
    projection_in,
    home_ref,
    send_ref,
    back_ref,
    projection_ref,
    tenant_ref,
    length_ref,
    admitted_ref,
    tenant_adapter_ref,
    adapter_slot_ref,
    token_ref,
    seen,
    query_ref,
    key_ref,
    value_ref,
    new_key_ref,
    new_value_ref,
    attended,
    score_ref,
    weight_ref,
    sems,
):
    rows = steps * heads
    total = requests * rows
    pairs = steps * requests
    width = key_ref.shape[2]
    context = key_ref.shape[1]
    features = heads * width
    scale = width ** (-0.5)
    copies = fetch_all(
        [
            (tenant_in, tenant_ref),
            (length_in, length_ref),
            (admitted_in, admitted_ref),
            (tenant_adapter_in, tenant_adapter_ref),
            (adapter_slot_in, adapter_slot_ref),
            (token_in, token_ref),
            (query_in, query_ref),
            (new_key_in, new_key_ref),
            (new_value_in, new_value_ref),
            (key_in, key_ref),
            (value_in, value_ref),
            (projection_in.at[pl.ds(0, projection_ref.shape[0])], projection_ref),
        ],
        sems,
    )
    for index in range(seen.shape[0]):
        seen[index] = 0
    for copy in copies[:9]:
        copy.wait()

    lane = iota((1, lanes), 1)
    place = iota((pairs, 1), 0)
    lane_of_pair = iota((1, pairs), 1)
    shared_row = iota((8, lanes), 0)
    shared_lane = iota((8, lanes), 1)
    flat_rows = jnp.zeros((pairs, 1), jnp.int32)
    flat_lanes = jnp.zeros((1, pairs), jnp.int32)
    scalars = jnp.zeros((pairs, lanes), f32)
    shared = jnp.zeros((8, lanes), f32)
    first_scalar = 3 * heads * (steps - 1)
    for r in range(requests):
        tenant = tenant_ref[r]
        tokens = token_ref[tenant]
        slot = adapter_slot_ref[tenant_adapter_ref[tenant]]
        holder = slot // adapters_held
        position = seen[holder]
        seen[holder] = position + 1
        flat = (holder * capacity + position) * steps
        flat_rows = jnp.where(place % requests == r, flat, flat_rows)
        flat_lanes = jnp.where(lane_of_pair % requests == r, flat, flat_lanes)
        tenant_parts = [tenant // 16, tenant % 16]
        admits = [admitted_ref[s, r] for s in range(steps)]
        own = [slot - holder * adapters_held] + tenant_parts + [tokens // 32, tokens % 32] + admits
        line = jnp.zeros((1, lanes), jnp.int32)
        for index, value in enumerate(own):
            line = jnp.where(lane == first_scalar + index, value, line)
        scalars = jnp.where(place % requests == r, line.astype(f32), scalars)
        column = jnp.zeros((8, lanes), jnp.int32)
        for index, value in enumerate(tenant_parts + [length_ref[r]] + admits):
            column = jnp.where(shared_row == index, value, column)
        shared = jnp.where(shared_lane == lanes // 2 + r, column.astype(f32), shared)
    flat_rows = flat_rows + place // requests
    flat_lanes = flat_lanes + lane_of_pair // requests
    back_ref[...] = one_hot(flat_rows, back_ref.shape)

    by_head = jnp.concatenate(
        [query_ref[:, h * width : (h + 1) * width] for h in range(heads)], axis=0
    )
    row = iota((total, total), 0)
    wanted = (row % heads) * pairs + ((row // heads) % steps) * requests + row // rows
    by_request = dot(one_hot(wanted, (total, total)), by_head).astype(bf16)
    new_scores = dot_t(by_request, new_key_ref[...]) * scale
    row = iota((total, 1), 0)
    new_column = iota((total, pairs), 1)
    by_step = [
        jnp.sum(
            jnp.where(new_column == j * requests + row // rows, new_scores, 0.0),
            axis=1,
            keepdims=True,
        )
        for j in range(steps)
    ]
    step_of_row = (row // heads) % steps
    own_score = by_step[0]
    for s in range(1, steps):
        own_score = jnp.where(step_of_row == s, by_step[s], own_score)
    own_place = new_column == step_of_row * requests + row // rows
    position = iota((rows, context), 1)
    copies[9].wait()
    for r in range(requests):
        block = slice(r * rows, (r + 1) * rows)
        scores = dot_t(by_request[block], key_ref[r]) * scale
        score_ref[block, :] = jnp.where(position < length_ref[r], scores, -jnp.inf)
    scores = score_ref[...]
    top = jnp.maximum(jnp.max(scores, axis=1, keepdims=True), own_score)
    weight = jnp.exp(scores - top)
    own_weight = jnp.exp(own_score - top)
    mass = jnp.sum(weight, axis=1, keepdims=True) + own_weight
    inverse = 1.0 / mass
    log_mass = top + jnp.log(mass)
    weight_ref[...] = (weight * inverse).astype(bf16)
    copies[10].wait()
    for r in range(requests):
        block = slice(r * rows, (r + 1) * rows)
        attended[block, :] = dot(weight_ref[block, :], value_ref[r])
    own_weights = jnp.where(own_place, own_weight * inverse, 0.0).astype(bf16)
    result = (attended[...] + dot(own_weights, new_value_ref[...])).astype(bf16)

    row = iota((total, total), 0)
    wanted = (row % requests) * rows + ((row // requests) % steps) * heads + row // pairs
    by_head = dot(one_hot(wanted, (total, total)), result).astype(bf16)
    for h in range(heads):
        home_ref[:, h * width : (h + 1) * width] = by_head[h * pairs : (h + 1) * pairs]
    home_ref[:, features : features + width] = new_value_ref[...]
    row = iota((total, 1), 0)
    lane = iota((total, lanes), 1)
    pieces = jnp.zeros((total, lanes), f32)
    for j in range(steps - 1):
        rest = by_step[j] - log_mass
        for piece in range(3):
            part = rest.astype(bf16).astype(f32)
            rest = rest - part
            target = (piece * (steps - 1) + j) * heads + row % heads
            pieces = jnp.where(lane == target, part, pieces)
    column = iota((pairs, total), 1)
    wanted = ((column // heads) % steps) * requests + column // rows
    gather = (wanted == iota((pairs, total), 0)).astype(f32).astype(bf16)
    scalars = scalars + dot(gather, pieces.astype(bf16))
    home_ref[:, features + width :] = scalars.astype(bf16)
    slots = send_ref.shape[0]
    pick = (iota((slots, pairs), 0) == flat_lanes).astype(f32).astype(bf16)
    block = features + width
    picked = dot(pick, home_ref[...])
    spread = (iota((slots, 8), 0) % 8 == iota((slots, 8), 1)).astype(f32).astype(bf16)
    send_ref[:, 0:block] = picked[:, 0:block].astype(bf16)
    integers = dot(spread, shared.astype(bf16))
    send_ref[:, block:] = (picked[:, block:] + integers).astype(bf16)
    copies[11].wait()


def combine_kernel(
    steps,
    heads,
    width,
    threshold,
    got_ref,
    home_ref,
    down_ref,
    weight_ref,
    weight_in,
    low_ref,
    theirs_ref,
    others_ref,
    final_ref,
    late_ref,
    rows_ref,
    sem,
):
    early = weight_ref.shape[0]
    copy = pltpu.make_async_copy(weight_in.at[pl.ds(early, late_ref.shape[0])], late_ref, sem)
    copy.start()
    slots, pairs = got_ref.shape[0], home_ref.shape[0]
    features = heads * width
    sent = features + width + lanes
    count = slots + pairs
    block = features + width
    requests = pairs // steps
    everyone = requests * (slots // 8)
    column = iota((lanes, everyone), 1)
    tile = (iota((lanes, everyone), 0) == lanes // 2 + column % requests).astype(f32).astype(bf16)
    column = iota((slots, everyone), 1)
    from_row = column // requests == iota((slots, everyone), 0) // 8
    tiled = jnp.where(from_row, dot(got_ref[:, block:], tile), 0.0).astype(bf16)
    kind = (iota((8, slots), 1) % 8 == iota((8, slots), 0)).astype(f32).astype(bf16)
    shared = dot(kind, tiled)
    tenants = shared[0:1] * 16.0 + shared[1:2]
    charge_rows = []
    for s in range(steps - 1):
        charge = shared[2:3] + (s + 1.0)
        upper = jnp.floor(charge * (1.0 / 16.0))
        admitted = shared[3 + s : 4 + s]
        charge_rows += [upper * admitted, (charge - upper * 16.0) * admitted]
    charge_rows += [jnp.zeros_like(tenants)] * (8 - len(charge_rows))
    charges = jnp.concatenate(charge_rows, axis=0).astype(bf16)

    scalars = jnp.concatenate(
        [got_ref[:, block:sent].astype(f32), home_ref[:, block:sent].astype(f32)], axis=0
    )
    first = 3 * heads * (steps - 1)
    tenant = scalars[:, first + 1 : first + 2] * 16.0 + scalars[:, first + 2 : first + 3]
    tokens = scalars[:, first + 3 : first + 4] * 32.0 + scalars[:, first + 4 : first + 5]
    same = (tenant == tenants).astype(f32).astype(bf16)
    grows = dot_t(same, charges)
    row = iota((count, 1), 0)
    step_of_row = jnp.where(row < slots, row % steps, (row - slots) // requests)
    served_now = jnp.zeros((count, 1), f32)
    served = []
    for s in range(steps):
        open_now = (tokens < threshold).astype(f32)
        flag = open_now * scalars[:, first + 5 + s : first + 6 + s]
        served.append(flag)
        served_now = jnp.where(step_of_row == s, flag, served_now)
        if s + 1 < steps:
            grow = grows[:, 2 * s : 2 * s + 1] * 16.0 + grows[:, 2 * s + 1 : 2 * s + 2]
            tokens = tokens + open_now * grow

    span = heads * (steps - 1)
    logs = scalars[:, 0:span] + scalars[:, span : 2 * span] + scalars[:, 2 * span : 3 * span]
    shown = [(served[j] > 0.5) & (step_of_row > j) for j in range(steps - 1)]
    by_step = [
        jnp.where(shown[j], logs[:, j * heads : (j + 1) * heads], -jnp.inf)
        for j in range(steps - 1)
    ]
    top = jnp.zeros((count, heads), f32)
    for j in range(steps - 1):
        top = jnp.maximum(top, by_step[j])
    old = jnp.exp(-top)
    new = [jnp.exp(by_step[j] - top) for j in range(steps - 1)]
    mass = old
    for j in range(steps - 1):
        mass = mass + new[j]
    inverse = served_now / mass
    old = old * inverse
    new = [weight * inverse for weight in new]
    values = jnp.concatenate(
        [got_ref[:, features:block], home_ref[:, features:block]], axis=0
    )
    first_row = jnp.where(row < slots, row - row % steps, slots + (row - slots) % requests)
    stride = jnp.where(row < slots, 1, requests)
    new_values = [
        dot(one_hot(first_row + stride * j, (count, count)), values) for j in range(steps - 1)
    ]
    for h in range(heads):
        part = slice(h * width, (h + 1) * width)
        rows = jnp.concatenate([got_ref[:, part], home_ref[:, part]], axis=0).astype(f32)
        rows = rows * old[:, h : h + 1]
        for j in range(steps - 1):
            rows = rows + new_values[j] * new[j][:, h : h + 1]
        rows = rows.astype(bf16)
        rows_ref[:, part] = rows[0:slots]
        final_ref[:, part] = rows[slots:]

    rank = down_ref.shape[1]
    every = down_ref.shape[0] * rank
    product = dot_t(rows_ref[...], down_ref[...].reshape(every, features))
    owner = (iota(product.shape, 1) // rank).astype(f32)
    product = jnp.where(owner == scalars[0:slots, first : first + 1], product, 0.0)
    folded = product[:, 0:lanes]
    for start in range(lanes, every, lanes):
        folded = folded + product[:, start : start + lanes]
    folded = folded + pltpu.roll(folded, rank, 1)
    half = slots // 2
    low_half = iota((half, lanes), 1) < rank
    low = jnp.where(low_half, folded[0:half], folded[half:])
    low_ref[...] = low
    copy.wait()
    for index, product in enumerate(project(1, first_blocks, final_ref, weight_ref, late_ref)):
        theirs_ref[:, index * features : (index + 1) * features] = product.astype(bf16)
    start = len(first_blocks) * features
    upper = low.astype(bf16)
    theirs_ref[:, start : start + lanes] = upper
    theirs_ref[:, start + lanes :] = (low - upper.astype(f32)).astype(bf16)
    for index, product in enumerate(project(1, other_blocks[:1], final_ref, weight_ref, late_ref)):
        others_ref[index] = product.astype(bf16)


def project(flip, wanted, rows_ref, weight_ref, late_ref):
    parts = lax.axis_size("z")
    width = weight_ref.shape[1] // (2 * parts)
    early = weight_ref.shape[0]
    core = lax.axis_index("core")
    mine = core if flip == 0 else 1 - core
    here = lax.axis_index("z")
    way = 2 * lax.rem(here, 2) - 1
    products = []
    for part in wanted:
        target = lax.rem(here + way * part + parts, parts)
        start = pl.multiple_of((2 * target + mine) * width, width)
        block = pl.ds(start, width)
        product = dot(rows_ref[:, 0:early], weight_ref[:, block])
        products.append(product + dot(rows_ref[:, early:], late_ref[:, block]))
    return products


def rest_kernel(rows_ref, weight_ref, late_ref, out_ref, others_ref):
    blocks = first_blocks + other_blocks
    for index, product in enumerate(project(0, blocks, rows_ref, weight_ref, late_ref)):
        out_ref[index] = product
    for index, product in enumerate(project(1, other_blocks[1:], rows_ref, weight_ref, late_ref)):
        others_ref[index] = product.astype(bf16)


def mix_kernel(low_ref, ours_ref, came_ref, next_ref, others_ref, low_out, first_out, others_out):
    count, _, width = first_out.shape
    start = count * width
    other = came_ref[:, start : start + lanes].astype(f32)
    other = other + came_ref[:, start + lanes :].astype(f32)
    low = (low_ref[...] + other).astype(bf16)
    for part in range(low_out.shape[0]):
        low_out[part] = low
    for index in range(count):
        came = came_ref[:, index * width : (index + 1) * width].astype(f32)
        first_out[index] = (ours_ref[index] + came).astype(bf16)
    others_out[0:1] = next_ref[...]
    others_out[1:] = others_ref[...]


def hop_kernel(first, ours_ref, others_ref, came_ref, out_ref):
    skip = len(first_blocks) + first
    for index in range(out_ref.shape[0]):
        here = ours_ref[skip + index] + others_ref[first + index].astype(f32)
        out_ref[index] = (came_ref[index].astype(f32) + here).astype(bf16)


def late_hop_kernel(first, ours_ref, others_ref, came_ref, after_ref, out_ref):
    hop_kernel(first, ours_ref, others_ref, came_ref, out_ref)


def up_kernel(first_scalar, parts_ref, held_ref, up_ref, out_ref):
    rank = up_ref.shape[1]
    every = up_ref.shape[0] * rank
    low = parts_ref[0].astype(f32)
    for part in range(1, parts_ref.shape[0]):
        low = low + parts_ref[part].astype(f32)
    other = pltpu.roll(low, rank, 1)
    first = iota(low.shape, 1) < rank
    low = jnp.concatenate(
        [jnp.where(first, low, other), jnp.where(first, other, low)], axis=0
    )
    wide = jnp.concatenate([low] * (every // lanes), axis=1)
    owner = (iota(wide.shape, 1) // rank).astype(f32)
    held = held_ref[:, first_scalar : first_scalar + 1].astype(f32)
    wide = jnp.where(owner == held, wide, 0.0).astype(bf16)
    out_ref[...] = dot(wide, up_ref[...].reshape(every, up_ref.shape[2])).astype(bf16)


def sum_kernel(ours_ref, others_ref, first_ref, second_ref, out_ref):
    total = ours_ref[0] + others_ref[0].astype(f32)
    out_ref[...] = total + first_ref[0].astype(f32) + second_ref[0].astype(f32)


def finish_kernel(base_ref, back_ref, term_ref, out_ref):
    term = dot(back_ref[...], term_ref[...])
    out_ref[...] = (base_ref[...] + adapter_scale * term).astype(bf16)


def per_device(
    queries,
    cache_keys,
    cache_values,
    new_keys,
    new_values,
    lengths,
    admitted,
    request_tenant,
    tenant_adapter,
    adapter_slot,
    tenant_tokens,
    out_weight,
    adapter_down_factor,
    adapter_up_factor,
):
    holders = lax.axis_size("batch")
    parts = lax.axis_size("z")
    steps, requests, features = queries.shape
    context, width = cache_keys.shape[1], cache_keys.shape[3]
    heads = features // width
    rows = steps * heads
    total = requests * rows
    pairs = steps * requests
    adapters_held, rank, _ = adapter_down_factor.shape
    every = adapters_held * rank
    threshold = float(3 * context)
    early = features * 4 // 8
    slots = holders * capacity * steps
    first_scalar = 3 * heads * (steps - 1)
    sent = features + width + lanes
    shape = jax.ShapeDtypeStruct

    home, send, back, weight = call(
        functools.partial(attend_kernel, steps, requests, heads, adapters_held),
        (
            shape((pairs, sent), bf16),
            shape((slots, sent), bf16),
            shape((pairs, slots), bf16),
            pltpu.VMEM((early, out_weight.shape[1]), bf16),
        ),
        [HBM] * 12,
        (VMEM,) * 4,
        4 * total * context * width,
        4 * cache_keys.size,
        [
            pltpu.SMEM((requests,), jnp.int32),
            pltpu.SMEM((requests,), jnp.int32),
            pltpu.SMEM((steps, requests), jnp.int32),
            pltpu.SMEM(tenant_adapter.shape, jnp.int32),
            pltpu.SMEM(adapter_slot.shape, jnp.int32),
            pltpu.SMEM(tenant_tokens.shape, jnp.int32),
            pltpu.SMEM((holders,), jnp.int32),
            pltpu.VMEM((pairs, features), bf16),
            pltpu.VMEM((requests, context, width), bf16),
            pltpu.VMEM((requests, context, width), bf16),
            pltpu.VMEM((pairs, width), bf16),
            pltpu.VMEM((pairs, width), bf16),
            pltpu.VMEM((total, width), f32),
            pltpu.VMEM((total, context), f32),
            pltpu.VMEM((total, context), bf16),
            pltpu.SemaphoreType.DMA((12,)),
        ],
        40 << 20,
    )(
        *map(
            in_hbm,
            (
                request_tenant,
                lengths,
                admitted,
                tenant_adapter,
                adapter_slot,
                tenant_tokens,
                queries.reshape(pairs, features),
                cache_keys.reshape(requests, context, width),
                cache_values.reshape(requests, context, width),
                new_keys.reshape(pairs, width),
                new_values.reshape(pairs, width),
                out_weight,
            ),
        )
    )
    got = lax.all_to_all(send, "batch", split_axis=0, concat_axis=0, tiled=True)
    weight = in_vmem(weight)
    two = shape((2, pairs, features), bf16)
    one = shape((1, pairs, features), bf16)
    six = shape((len(other_blocks), pairs, features), bf16)
    blocks = shape((parts, pairs, features), f32)
    low, theirs, following, final, late = call(
        functools.partial(combine_kernel, steps, heads, width, threshold),
        (
            shape((slots // 2, lanes), f32),
            shape((pairs, 2 * features + 2 * lanes), bf16),
            one,
            shape((pairs, features), bf16),
            pltpu.VMEM((features - early, out_weight.shape[1]), bf16),
        ),
        [VMEM] * 4 + [HBM],
        (VMEM,) * 5,
        2 * slots * features * every,
        out_weight.size,
        [pltpu.VMEM((slots, features), bf16), pltpu.SemaphoreType.DMA],
    )(got, home, adapter_down_factor, weight, in_hbm(out_weight))
    swap = [(0, 1), (1, 0)]
    theirs = lax.ppermute(theirs, "core", swap)
    ours, others = call(
        rest_kernel,
        (blocks, shape((len(other_blocks) - 1, pairs, features), bf16)),
        [VMEM] * 3,
        (VMEM,) * 2,
        pairs * out_weight.size,
        out_weight.size,
    )(final, weight, in_vmem(late))
    low, sums, others = call(
        mix_kernel,
        (shape((parts, slots // 2, lanes), bf16), two, six),
        [VMEM] * 5,
        (VMEM,) * 3,
        2 * two.size,
        8 * two.size,
    )(low, ours, theirs, following, others)
    others = lax.ppermute(others, "core", swap)
    low = lax.all_to_all(low, "z", split_axis=0, concat_axis=0, tiled=True)

    def hop(kernel, first, out, *args):
        return call(
            functools.partial(kernel, first),
            out,
            [VMEM] * 3 + [HBM] * (len(args) - 3),
            VMEM,
            out.size,
            6 * out.size,
        )(*args)

    even = [(i, i + 1 - 2 * (i % 2)) for i in range(parts)]
    odd = [(i, (i - 1 + 2 * (i % 2)) % parts) for i in range(parts)]
    sums = lax.ppermute(sums, "z", odd)
    sums = lax.ppermute(hop(hop_kernel, 0, two, ours, others, sums), "z", even)
    term = call(
        functools.partial(up_kernel, first_scalar),
        shape((slots, features), bf16),
        [VMEM] * 3,
        VMEM,
        2 * slots * features * every,
        4 * slots * features,
    )(low, got[:, features + width : sent], adapter_up_factor)
    sums = hop(late_hop_kernel, 2, two, ours, others, sums, term)
    sums = lax.ppermute(sums, "z", odd)
    last = lax.ppermute(hop(hop_kernel, 4, one, ours, others, sums), "z", even)
    term = lax.all_to_all(term, "batch", split_axis=0, concat_axis=0, tiled=True)
    base = call(
        sum_kernel,
        shape((pairs, features), f32),
        [VMEM] * 4,
        VMEM,
        4 * one.size,
        12 * one.size,
    )(ours[-1:], others[-1:], sums[1:], last)
    out = call(
        finish_kernel,
        shape((pairs, features), bf16),
        [VMEM] * 3,
        VMEM,
        2 * pairs * slots * features,
        10 * one.size,
    )(base, back, term)
    return out.reshape(steps, requests, features)


def solution(mesh):
    batch, tensor = mesh.shape["batch"], mesh.shape["tensor"]
    split = Mesh(mesh.devices.reshape(batch, tensor // 2, 2), ("batch", "z", "core"))
    tensor_axes = ("z", "core")
    placed = (
        P(None, "batch", tensor_axes),
        P("batch", None, tensor_axes, None),
        P("batch", None, tensor_axes, None),
        P(None, "batch", tensor_axes, None),
        P(None, "batch", tensor_axes, None),
        P("batch"),
        P(None, "batch"),
        P("batch"),
        P(),
        P(),
        P(),
        P(tensor_axes, None),
        P("batch", None, tensor_axes),
        P("batch", None, tensor_axes),
    )
    return jax.shard_map(
        per_device,
        mesh=split,
        in_specs=placed,
        out_specs=P(None, "batch", tensor_axes),
        check_vma=False,
    )
```
